128 devices in a mesh: row: 8 (over y, x_hi), col: 16 (over z, x_lo, core).
Axes of the slice: x: 4 (x_hi: 2, x_lo: 2; x = x_hi * 2 + x_lo), y: 4, z: 4, core: 2. Of those that a mesh axis runs over, the one named last changes fastest.
Arguments:
- ham_tiles: float32 [8, 16, 320, 128, 128], P('row', 'col'), may hold values from -0.0625 to 0.0625
- tile_list: int32 [8, 16, 320, 2], P('row', 'col'), may hold values from 0 to 63, as said below
- tile_count: int32 [8, 16], P('row', 'col'), may hold values from 1 to 320, as said below
- basis_block: float32 [16, 65536], P(None, ('row', 'col')), may hold values from -6 to 6
- residual_block: float32 [16, 65536], P(None, ('row', 'col')), may hold values from -6 to 6
Outputs:
- h_basis: float32 [16, 65536], P(None, ('row', 'col'))
- h_residual: float32 [16, 65536], P(None, ('row', 'col'))
The draws below stay inside these ranges and needn't reach their ends.
Inputs may be any that keep to these rules, and one draw needn't show every extreme that they name: `tile_list`: entry 0 is a block row within the grid row, below 64; entry 1 a block column within the grid column, below 32. Live slots name distinct blocks with global row block at most the global column block; slots past the count name arbitrary blocks in range. `tile_count`: each device's count lies between half and all of its share of 320 in proportion to its upper-triangle slots, never above its distinct upper blocks; devices with the most upper-triangle slots hold exactly 320.
All inputs are finite; a program needn't handle non-finite values.
Results may differ from the reference program's by a relative error of at most 0.0003.
Values sent between devices are 32-bit elements; how exact they have to be, the bound alone decides.
A program may use at most 128 MiB of HBM per device.

```python
import jax
import jax.numpy as jnp
from jax import lax

TILE = 128
VEC = 16
BP = 4
MAXT = 320
NB = 512
BR = 64
NSTATES = 65536
N_ROW = 8
N_COL = 16


def tile_layout(key):
    slots = BR * N_ROW * BP
    row_ids = jnp.arange(N_ROW, dtype=jnp.int32)[:, None, None, None]
    col_ids = jnp.arange(N_COL, dtype=jnp.int32)[None, :, None, None]
    local_rows = jnp.arange(BR, dtype=jnp.int32)[None, None, :, None]
    local_cols = jnp.arange(N_ROW * BP, dtype=jnp.int32)[None, None, None, :]
    global_row = row_ids * BR + local_rows
    global_col = local_cols // BP * BR + col_ids * BP + local_cols % BP
    upper = (global_row <= global_col).reshape(N_ROW, N_COL, slots)
    valid = jnp.sum(upper.astype(jnp.int32), axis=-1)
    most = jnp.max(valid)
    ceiling = jnp.maximum(1, MAXT * valid // most).astype(jnp.int32)
    floor_count = jnp.maximum(1, ceiling // 2).astype(jnp.int32)
    count_key = jax.random.fold_in(key, 7)
    drawn = jax.random.randint(count_key, (N_ROW, N_COL), floor_count, ceiling + 1, dtype=jnp.int32)
    counts = jnp.where(valid == most, jnp.int32(MAXT), drawn).astype(jnp.int32)
    scores_raw = jax.random.randint(key, (N_ROW, N_COL, slots), 0, 65536, dtype=jnp.int32)
    slot_ids = jnp.arange(slots, dtype=jnp.int32)
    scores = jnp.where(upper, scores_raw * slots + slot_ids, -1 - slot_ids)
    _, chosen = jax.lax.top_k(scores, MAXT)
    chosen = chosen.astype(jnp.int32)
    listing = jnp.stack([chosen // (N_ROW * BP), chosen % (N_ROW * BP)], axis=-1).astype(jnp.int32)
    return (listing, counts)


def draw_tile_list(key, part):
    listing, counts = tile_layout(key)
    return listing


def draw_tile_count(key, part):
    listing, counts = tile_layout(key)
    return counts


def steps_of(stream_key, extent, shards, least, top_value):
    gain = 1.0
    for axis_at, shards_of in shards:
        steps = jax.random.uniform(jax.random.fold_in(jax.random.fold_in(stream_key, 6), axis_at), (shards_of,), jnp.float32, least / len(shards), top_value / len(shards))
        gain = gain * jnp.repeat(jnp.exp(steps), extent[axis_at] // shards_of).reshape((-1,) + (1,) * (len(extent) - 1 - axis_at))
    return gain


def centred(stream_key, shape, deviation, limit, shards=(), kind=jnp.bfloat16):
    level = steps_of(stream_key, shape, shards, -0.22, 0.18) if shards else 1.0
    values = jax.random.normal(stream_key, shape, jnp.float32) * deviation * level
    return jnp.minimum(jnp.maximum(values, -limit), limit).astype(kind)


def setup_inputs(seed: int = 0) -> dict:
    keys = jax.random.split(jax.random.key(seed), 6)
    return {
        "ham_tiles": centred(keys[0], (N_ROW, N_COL, MAXT, TILE, TILE), (TILE * BP * 16) ** -0.5, 0.0625, ((0, 8), (1, 16)), jnp.float32),
        "tile_list": draw_tile_list(jax.random.fold_in(keys[5], 71), 0),
        "tile_count": draw_tile_count(jax.random.fold_in(keys[5], 71), 0),
        "basis_block": centred(keys[3], (VEC, NSTATES), 1.0, 6.0, ((1, 128),), jnp.float32),
        "residual_block": centred(keys[4], (VEC, NSTATES), 1.0, 6.0, ((1, 128),), jnp.float32),
    }


def reference(ham_tiles, tile_list, tile_count, basis_block, residual_block):
    panel = jnp.concatenate([basis_block, residual_block], axis=0)
    width = panel.shape[0]
    blocks = panel.reshape(width, NB, TILE)
    flat_tiles = ham_tiles.reshape(N_ROW * N_COL, MAXT, TILE, TILE)
    flat_list = tile_list.reshape(N_ROW * N_COL, MAXT, 2)
    flat_count = tile_count.reshape(N_ROW * N_COL)
    device_ids = jnp.arange(N_ROW * N_COL, dtype=jnp.int32)

    def step(carry, items):
        tile_data, listing, count, device = items
        row_index = device // N_COL
        col_index = device % N_COL
        local_row = listing[:, 0]
        local_col = listing[:, 1]
        global_row = (row_index * BR + local_row).astype(jnp.int32)
        global_col = ((local_col // BP) * BR + col_index * BP + local_col % BP).astype(jnp.int32)
        live = jnp.arange(MAXT, dtype=jnp.int32) < count
        is_diag = global_row == global_col
        masked = jnp.where(live[:, None, None], tile_data, jnp.float32(0.0))
        forward = jnp.where(is_diag[:, None, None], 0.5 * (masked + jnp.swapaxes(masked, 1, 2)), masked)
        transposed = jnp.where(is_diag[:, None, None], jnp.float32(0.0), masked)
        from_cols = blocks[:, global_col]
        from_rows = blocks[:, global_row]
        fwd_terms = jnp.einsum('vtb,tab->vta', from_cols, forward, precision=lax.Precision.HIGHEST)
        tr_terms = jnp.einsum('vta,tab->vtb', from_rows, transposed, precision=lax.Precision.HIGHEST)
        carry = carry.at[:, global_row].add(fwd_terms)
        carry = carry.at[:, global_col].add(tr_terms)
        return carry, None

    start = jnp.zeros((width, NB, TILE), jnp.float32)
    result, _ = lax.scan(step, start, (flat_tiles, flat_list, flat_count, device_ids))
    result = result.reshape(width, NB * TILE)
    return result[:VEC], result[VEC:]
```

```python
import functools

import jax
import jax.numpy as jnp
from jax import lax
from jax.experimental import pallas as pl
from jax.experimental.pallas import tpu as pltpu
from jax.sharding import PartitionSpec as P

MESH = pl.DeviceIdType.MESH
TILE = 128
BP = 4
NT = (((1,), (1,)), ((), ()))
NN = (((1,), (0,)), ((), ()))
BF = jnp.bfloat16
F32 = jnp.float32
I32 = jnp.int32


def split2(value):
    hi = value.astype(BF)
    lo = (value - hi.astype(F32)).astype(BF)
    return hi, lo


def put_operand(dst, index, block):
    rows = block.shape[0]
    hi, lo = split2(block)
    dst[index, :rows, :TILE] = hi
    dst[index, :rows, TILE:] = hi
    dst[index, rows:, :TILE] = lo
    dst[index, rows:, TILE:] = jnp.zeros_like(lo)


def row_of(column, spot):
    return jnp.sum(jnp.where(spot, column, 0), axis=0, keepdims=True)


def sorted_lists(key, other, weight2, iota0, iota1, slots):
    tagged = key * 512 + iota0[:, :1]
    tagged_row = row_of(tagged, iota0 == iota1)
    real = iota1 < slots
    rank = jnp.sum(jnp.where((tagged_row < tagged) & real, 1, 0), axis=1, keepdims=True)
    earlier = (tagged_row < tagged) & real & (tagged_row >= key * 512)
    repeats = jnp.minimum(
        jnp.sum(jnp.where(earlier, 1, 0), axis=1, keepdims=True), 1
    )
    place = rank == iota1
    return (
        row_of(iota0[:, :1], place),
        row_of(other, place),
        row_of(repeats, place),
        row_of(weight2, place),
    )


def segment_ends(key, lanes):
    last = jnp.sum(jnp.where(key <= lanes, 1, 0), axis=0, keepdims=True) - 1
    some = jnp.minimum(jnp.sum(jnp.where(key == lanes, 1, 0), axis=0, keepdims=True), 1)
    return jnp.maximum(last, 0), some


def kernel(
    n_row,
    n_col,
    unroll,
    chunks,
    list_ref,
    count_ref,
    basis_ref,
    residual_ref,
    tiles_ref,
    out_basis,
    out_residual,
    raw,
    halves,
    running,
    row_raw,
    col_raw,
    row_x,
    col_x,
    row_part,
    from_twin,
    from_row,
    col_part,
    from_col,
    lists_v,
    lists_s,
    marks_v,
    marks_s,
    tile_sem,
    list_sem,
    far_send,
    far_recv,
    twin_send,
    twin_recv,
    up_send,
    up_recv,
    fold_sem,
    back_send,
    back_recv,
    down_send,
    down_recv,
):
    slots = halves.shape[0]
    width = row_raw.shape[2]
    half = width // 2
    chips = n_col // 2
    per = slots // chunks
    r = lax.axis_index("row")
    c = lax.axis_index("col")
    core = c % 2
    chip = c // 2
    twin = chip * 2 + 1 - core
    zs, z, xl = chips // 2, chip // 2, chip % 2

    def chip_at(d):
        return ((z + d // 2) % zs) * 2 + (xl + d % 2) % 2

    def tile_copy(k):
        part = pl.ds(k * per, per)
        return pltpu.make_async_copy(
            tiles_ref.at[0, 0, part], raw.at[part], tile_sem.at[k]
        )

    def remote(src, dst, send, recv, row, col):
        return pltpu.make_async_remote_copy(
            src_ref=src,
            dst_ref=dst,
            send_sem=send,
            recv_sem=recv,
            device_id=(row, col),
            device_id_type=MESH,
        )

    for k in range(chunks):
        tile_copy(k).start()

    for b in range(BP):
        columns = slice(b * TILE, (b + 1) * TILE)
        row_raw[c, b, :half] = basis_ref[:, columns]
        row_raw[c, b, half:] = residual_ref[:, columns]
        col_raw[r, b, :half] = basis_ref[:, columns]
        col_raw[r, b, half:] = residual_ref[:, columns]
    for g in range(n_row):

        @pl.when(g < r)
        def _():
            col_raw[g] = jnp.zeros(col_raw.shape[1:], F32)

    barrier = pltpu.get_barrier_semaphore()
    for d in range(1, n_row):
        pl.semaphore_signal(
            barrier, inc=1, device_id=((r + d) % n_row, c), device_id_type=MESH
        )
    pl.semaphore_signal(barrier, inc=1, device_id=(r, twin), device_id_type=MESH)
    for d in range(1, chips):
        pl.semaphore_signal(
            barrier, inc=1, device_id=(r, chip_at(d) * 2 + core), device_id_type=MESH
        )
    pl.semaphore_wait(barrier, n_row - 1 + 1 + chips - 1)

    def up_copy(d):
        return remote(
            col_raw.at[r], col_raw.at[r], up_send.at[d], up_recv.at[r], (r + n_row - d) % n_row, c
        )

    def up_arrival(g):
        return remote(col_raw.at[g], col_raw.at[g], up_send.at[0], up_recv.at[g], r, twin)

    def far_copy(d):
        return remote(
            row_raw.at[c],
            row_raw.at[c],
            far_send.at[d],
            far_recv.at[chip],
            r,
            chip_at(d) * 2 + core,
        )

    def far_arrival(q):
        piece = row_raw.at[q * 2 + core]
        return remote(piece, piece, far_send.at[0], far_recv.at[q], r, twin)

    def twin_copy(q):
        piece = row_raw.at[q * 2 + core]
        return remote(piece, piece, twin_send.at[q], twin_recv.at[q], r, twin)

    def twin_arrival(q):
        piece = row_raw.at[q * 2 + 1 - core]
        return remote(piece, piece, twin_send.at[0], twin_recv.at[q], r, twin)

    for d in range(n_row - 1, 0, -1):

        @pl.when(d <= r)
        def _():
            up_copy(d).start()

    twin_copy(chip).start()
    for d in range(1, chips):
        far_copy(d).start()

    padded = lists_v.shape[1]
    iota0 = lax.broadcasted_iota(I32, (slots, padded), 0)
    iota1 = lax.broadcasted_iota(I32, (slots, padded), 1)
    listing = list_ref[0, 0]
    local_row = listing[:, 0:1]
    local_col = listing[:, 1:2]
    slot = iota0[:, :1]
    diagonal = (r * (n_col * BP) + local_row) == (
        (local_col // BP) * (n_col * BP) + c * BP + local_col % BP
    )
    weight2 = jnp.where(slot < count_ref[0, 0], jnp.where(diagonal, 1, 2), 0)
    by_row = sorted_lists(local_row, local_col, weight2, iota0, iota1, slots)
    by_col = sorted_lists(local_col, local_row, weight2, iota0, iota1, slots)
    lanes = lax.broadcasted_iota(I32, (slots, TILE), 1)
    row_end, row_some = segment_ends(local_row, lanes)
    col_end, col_some = segment_ends(local_col, lanes)
    for k, (order, other, again, weight) in enumerate((by_row, by_col)):
        lists_v[2 * k : 2 * k + 1] = order
        lists_v[2 * k + 1 : 2 * k + 2] = other
        marks_v[2 * k : 2 * k + 1] = again.astype(F32)
        marks_v[2 * k + 1 : 2 * k + 2] = weight.astype(F32) * 0.5
    lists_v[4:5, :TILE] = row_end
    lists_v[5:6, :TILE] = col_end
    marks_v[4:5, :TILE] = row_some.astype(F32)
    marks_v[5:6, :TILE] = col_some.astype(F32)
    lists_copy = pltpu.make_async_copy(lists_v, lists_s, list_sem.at[0])
    marks_copy = pltpu.make_async_copy(marks_v, marks_s, list_sem.at[1])
    lists_copy.start()
    marks_copy.start()

    group = 8

    @pl.loop(0, chunks)
    def _(k):
        tile_copy(k).wait()

        @pl.loop(0, per // group)
        def _(s):
            for u in range(group):
                t = k * per + s * group + u
                hi, lo = split2(raw[t])
                halves[t, :TILE] = hi
                halves[t, TILE:] = lo

    lists_copy.wait()
    marks_copy.wait()

    for g in range(1, n_row):

        @pl.when(g > r)
        def _():
            up_arrival(g).wait_recv()

    @pl.loop(0, n_row)
    def _(g):
        for b in range(BP):
            put_operand(col_x, g * BP + b, col_raw[g, b])

    def products(which, operand, forward, between):
        order_at, other_at = 2 * which, 2 * which + 1

        def body(s, total):
            between(s)
            for u in range(unroll):
                k = s * unroll + u
                t = lists_s[order_at, k]
                o = lists_s[other_at, k]
                tile = halves[t]
                if forward:
                    tile = jnp.concatenate([tile[:TILE], tile[TILE:]], axis=1)
                term = lax.dot_general(
                    operand[o], tile, NT if forward else NN, preferred_element_type=F32
                )
                term = term[:width] + term[width:]
                total = total * marks_s[2 * which, k] + term * marks_s[2 * which + 1, k]
                running[k] = total
            return total

        lax.fori_loop(0, slots // unroll, body, jnp.zeros((width, TILE), F32))

    def hand_over(s):
        @pl.when((s >= 1) & (s < chips))
        def _():
            q = chip_at(s)
            far_arrival(q).wait_recv()
            twin_copy(q).start()

    assert slots // unroll >= chips
    products(0, col_x, True, hand_over)

    @pl.loop(0, n_col)
    def _(p):
        for b in range(BP):
            k = lists_s[4, p * BP + b]
            row_part[p % 2, p // 2, b] = running[k] * marks_s[4, p * BP + b]

    fold = remote(
        row_part.at[1 - core], from_twin, fold_sem.at[0], fold_sem.at[1], r, twin
    )
    fold.start()

    for q in range(chips):
        twin_arrival(q).wait_recv()

    @pl.loop(0, n_col)
    def _(p):
        for b in range(BP):
            put_operand(row_x, p * BP + b, row_raw[p, b])

    def back_copy(d):
        q = chip_at(d)
        return remote(
            row_part.at[core, q],
            from_row.at[chip],
            back_send.at[d],
            back_recv.at[chip],
            r,
            q * 2 + core,
        )

    def back_arrival(d):
        q = chip_at(d)
        return remote(
            from_row.at[q], from_row.at[q], back_send.at[0], back_recv.at[q], r, twin
        )

    def fold_in(s):
        @pl.when(s == 2)
        def _():
            fold.wait_recv()
            for d in range(chips):
                q = chip_at(d)
                row_part[core, q] = row_part[core, q] + from_twin[q]
                if d > 0:
                    back_copy(d).start()

    products(1, row_x, False, fold_in)

    @pl.loop(0, n_row)
    def _(g):
        for b in range(BP):
            k = lists_s[5, g * BP + b]
            col_part[g, b] = running[k] * marks_s[5, g * BP + b]

    def down_copy(d):
        g = (r + d) % n_row
        return remote(
            col_part.at[g], from_col.at[r], down_send.at[d], down_recv.at[r], g, c
        )

    def down_arrival(g):
        return remote(
            from_col.at[g], from_col.at[g], down_send.at[0], down_recv.at[g], r, twin
        )

    for d in range(n_row - 1, 0, -1):

        @pl.when(r + d < n_row)
        def _():
            down_copy(d).start()

    row_part[core, chip] = row_part[core, chip] + col_part[r]
    for d in range(1, chips):
        back_arrival(d).wait_recv()
        row_part[core, chip] = row_part[core, chip] + from_row[chip_at(d)]
    for g in range(n_row - 1):

        @pl.when(g < r)
        def _():
            down_arrival(g).wait_recv()
            row_part[core, chip] = row_part[core, chip] + from_col[g]

    for b in range(BP):
        columns = slice(b * TILE, (b + 1) * TILE)
        out_basis[:, columns] = row_part[core, chip, b, :half]
        out_residual[:, columns] = row_part[core, chip, b, half:]

    for d in range(1, n_row):

        @pl.when(d <= r)
        def _():
            up_copy(d).wait_send()

        @pl.when(r + d < n_row)
        def _():
            down_copy(d).wait_send()

    for d in range(1, chips):
        far_copy(d).wait_send()
        back_copy(d).wait_send()
    for q in range(chips):
        twin_copy(q).wait_send()
    fold.wait_send()


def solution(mesh):
    n_row, n_col = mesh.shape["row"], mesh.shape["col"]
    chips = n_col // 2

    def local(ham_tiles, tile_list, tile_count, basis_block, residual_block):
        slots = ham_tiles.shape[2]
        width = 2 * basis_block.shape[0]
        padded = -(-slots // TILE) * TILE
        unroll = 20 if slots % 20 == 0 else 4
        chunks = 8
        vmem = pl.BlockSpec(memory_space=pltpu.VMEM)
        dma = pltpu.SemaphoreType.DMA
        piece = (BP, width, TILE)
        shape = jax.ShapeDtypeStruct(basis_block.shape, F32)
        return pl.pallas_call(
            functools.partial(kernel, n_row, n_col, unroll, chunks),
            out_shape=(shape, shape),
            in_specs=[
                vmem,
                pl.BlockSpec(memory_space=pltpu.SMEM),
                vmem,
                vmem,
                pl.BlockSpec(memory_space=pl.ANY),
            ],
            out_specs=(vmem, vmem),
            scratch_shapes=[
                pltpu.VMEM((slots, TILE, TILE), F32),
                pltpu.VMEM((slots, 2 * TILE, TILE), BF),
                pltpu.VMEM((slots, width, TILE), F32),
                pltpu.VMEM((n_col,) + piece, F32),
                pltpu.VMEM((n_row,) + piece, F32),
                pltpu.VMEM((n_col * BP, 2 * width, 2 * TILE), BF),
                pltpu.VMEM((n_row * BP, 2 * width, 2 * TILE), BF),
                pltpu.VMEM((2, chips) + piece, F32),
                pltpu.VMEM((chips,) + piece, F32),
                pltpu.VMEM((chips,) + piece, F32),
                pltpu.VMEM((n_row,) + piece, F32),
                pltpu.VMEM((n_row,) + piece, F32),
                pltpu.VMEM((8, padded), I32),
                pltpu.SMEM((8, padded), I32),
                pltpu.VMEM((8, padded), F32),
                pltpu.SMEM((8, padded), F32),
                dma((chunks,)),
                dma((2,)),
                dma((chips,)),
                dma((chips,)),
                dma((chips,)),
                dma((chips,)),
                dma((n_row,)),
                dma((n_row,)),
                dma((2,)),
                dma((chips,)),
                dma((chips,)),
                dma((n_row,)),
                dma((n_row,)),
            ],
            compiler_params=pltpu.CompilerParams(
                collective_id=0,
                has_side_effects=True,
                vmem_limit_bytes=60 * 2**20,
            ),
        )(tile_list, tile_count, basis_block, residual_block, ham_tiles)

    return jax.shard_map(
        local,
        mesh=mesh,
        in_specs=(
            P("row", "col", None, None, None),
            P("row", "col", None, None),
            P("row", "col"),
            P(None, ("row", "col")),
            P(None, ("row", "col")),
        ),
        out_specs=(P(None, ("row", "col")), P(None, ("row", "col"))),
        check_vma=False,
    )
```

```python
import functools

import jax
import jax.numpy as jnp
from jax import lax
from jax.experimental import pallas as pl
from jax.experimental.pallas import tpu as pltpu
from jax.sharding import PartitionSpec as P

MESH = pl.DeviceIdType.MESH
TILE = 128
BP = 4
NT = (((1,), (1,)), ((), ()))
NN = (((1,), (0,)), ((), ()))
BF = jnp.bfloat16
F32 = jnp.float32
I32 = jnp.int32


def split2(value):
    hi = value.astype(BF)
    lo = (value - hi.astype(F32)).astype(BF)
    return hi, lo


def put_operand(dst, index, block):
    rows = block.shape[0]
    hi, lo = split2(block)
    dst[index, :rows, :TILE] = hi
    dst[index, :rows, TILE:] = hi
    dst[index, rows:, :TILE] = lo
    dst[index, rows:, TILE:] = jnp.zeros_like(lo)


def row_of(column, spot):
    return jnp.sum(jnp.where(spot, column, 0), axis=0, keepdims=True)


def column_of(row, spot):
    return jnp.sum(jnp.where(spot, row, 0), axis=1, keepdims=True)


def sorted_lists(key, other, weight2, iota0, iota1, slots):
    tagged = key * 512 + iota0[:, :1]
    tagged_row = row_of(tagged, iota0 == iota1)
    before = (tagged_row < tagged) & (iota1 < slots)
    rank = jnp.sum(jnp.where(before, 1, 0), axis=1, keepdims=True)
    earlier = before & (tagged_row >= key * 512)
    repeats = jnp.minimum(
        jnp.sum(jnp.where(earlier, 1, 0), axis=1, keepdims=True), 1
    )
    place = rank == iota1
    return (
        row_of(iota0[:, :1], place),
        row_of(other, place),
        row_of(repeats, place),
        row_of(weight2, place),
    )


def segment_ends(key, lanes):
    last = jnp.sum(jnp.where(key <= lanes, 1, 0), axis=0, keepdims=True) - 1
    some = jnp.minimum(jnp.sum(jnp.where(key == lanes, 1, 0), axis=0, keepdims=True), 1)
    return jnp.maximum(last, 0), some


def kernel(
    n_row,
    n_col,
    unroll,
    chunks,
    list_ref,
    count_ref,
    basis_ref,
    residual_ref,
    tiles_ref,
    out,
    raw,
    halves,
    running,
    row_raw,
    col_raw,
    row_x,
    col_x,
    row_part,
    from_twin,
    from_row,
    col_part,
    from_col,
    lists_v,
    lists_s,
    marks_v,
    marks_s,
    tile_sem,
    list_sem,
    far_send,
    far_recv,
    twin_send,
    twin_recv,
    up_send,
    up_recv,
    fold_sem,
    back_send,
    back_recv,
    down_send,
    down_recv,
):
    slots = halves.shape[0]
    width = row_raw.shape[2]
    half = width // 2
    chips = n_col // 2
    per = slots // chunks
    blocks = n_col * BP
    r = lax.axis_index("row")
    c = lax.axis_index("col")
    core = c % 2
    chip = c // 2
    twin = chip * 2 + 1 - core

    upper = (n_row - 1 - r) * (BP * blocks) + BP * BP * c + BP * (BP + 1) // 2
    most = (n_row - 1) * (BP * blocks) + BP * BP * (n_col - 1) + BP * (BP + 1) // 2
    bound = jnp.minimum(slots * upper // most + 1, slots)
    steps = (bound + unroll - 1) // unroll
    parts = (bound + per - 1) // per

    def tile_copy(k):
        part = pl.ds(k * per, per)
        return pltpu.make_async_copy(
            tiles_ref.at[0, 0, part], raw.at[part], tile_sem.at[k]
        )

    def remote(src, dst, send, recv, row, col):
        return pltpu.make_async_remote_copy(
            src_ref=src,
            dst_ref=dst,
            send_sem=send,
            recv_sem=recv,
            device_id=(row, col),
            device_id_type=MESH,
        )

    @pl.loop(0, parts)
    def _(k):
        tile_copy(k).start()

    for b in range(BP):
        columns = slice(b * TILE, (b + 1) * TILE)
        row_raw[c, b, :half] = basis_ref[:, columns]
        row_raw[c, b, half:] = residual_ref[:, columns]
        col_raw[r, b, :half] = basis_ref[:, columns]
        col_raw[r, b, half:] = residual_ref[:, columns]
    for g in range(n_row):

        @pl.when(g < r)
        def _():
            col_raw[g] = jnp.zeros(col_raw.shape[1:], F32)

    barrier = pltpu.get_barrier_semaphore()

    @pl.loop(r + 1, n_row)
    def _(g):
        pl.semaphore_signal(barrier, inc=1, device_id=(g, c), device_id_type=MESH)

    @pl.loop(chip + 1, chips)
    def _(q):
        pl.semaphore_signal(
            barrier, inc=1, device_id=(r, q * 2 + core), device_id_type=MESH
        )

    @pl.when(core == 0)
    def _():
        pl.semaphore_signal(barrier, inc=1, device_id=(r, twin), device_id_type=MESH)

    @pl.when(r + chip + core > 0)
    def _():
        pl.semaphore_wait(barrier, r + chip + core)

    def up_copy(g):
        return remote(col_raw.at[r], col_raw.at[r], up_send.at[g], up_recv.at[r], g, c)

    def up_arrival(g):
        return remote(col_raw.at[g], col_raw.at[g], up_send.at[0], up_recv.at[g], r, twin)

    def far_copy(q):
        return remote(
            row_raw.at[c], row_raw.at[c], far_send.at[q], far_recv.at[chip], r, q * 2 + core
        )

    def far_arrival(q):
        piece = row_raw.at[q * 2 + core]
        return remote(piece, piece, far_send.at[0], far_recv.at[q], r, twin)

    def twin_copy(q):
        piece = row_raw.at[q * 2 + core]
        return remote(piece, piece, twin_send.at[q], twin_recv.at[q], r, twin)

    def twin_arrival(q):
        piece = row_raw.at[q * 2 + 1 - core]
        return remote(piece, piece, twin_send.at[0], twin_recv.at[q], r, twin)

    @pl.loop(0, r)
    def _(g):
        up_copy(g).start()

    @pl.when(core == 1)
    def _():
        twin_copy(chip).start()

    @pl.loop(0, chip)
    def _(q):
        far_copy(q).start()

    padded = lists_v.shape[1]
    iota0 = lax.broadcasted_iota(I32, (slots, padded), 0)
    iota1 = lax.broadcasted_iota(I32, (slots, padded), 1)
    listing = jnp.concatenate(
        [list_ref[0, 0], jnp.zeros((2, padded - slots), I32)], axis=1
    )
    local_row = column_of(listing[0:1], iota0 == iota1)
    local_col = column_of(listing[1:2], iota0 == iota1)
    live = iota0[:, :1] < count_ref[0, 0]
    diagonal = (r * (n_col * BP) + local_row) == (
        (local_col // BP) * (n_col * BP) + c * BP + local_col % BP
    )
    weight2 = jnp.where(live, jnp.where(diagonal, 1, 2), 0)
    row_key = jnp.where(live, local_row, blocks)
    col_key = jnp.where(live, local_col, blocks)
    by_row = sorted_lists(row_key, local_col, weight2, iota0, iota1, slots)
    by_col = sorted_lists(col_key, local_row, weight2, iota0, iota1, slots)
    lanes = lax.broadcasted_iota(I32, (slots, TILE), 1)
    row_end, row_some = segment_ends(row_key, lanes)
    col_end, col_some = segment_ends(col_key, lanes)
    for k, (order, other, again, weight) in enumerate((by_row, by_col)):
        lists_v[2 * k : 2 * k + 1] = order
        lists_v[2 * k + 1 : 2 * k + 2] = other
        marks_v[2 * k : 2 * k + 1] = again.astype(F32)
        marks_v[2 * k + 1 : 2 * k + 2] = weight.astype(F32) * 0.5
    lists_v[4:5, :TILE] = row_end
    lists_v[5:6, :TILE] = col_end
    marks_v[4:5, :TILE] = row_some.astype(F32)
    marks_v[5:6, :TILE] = col_some.astype(F32)
    lists_copy = pltpu.make_async_copy(lists_v, lists_s, list_sem.at[0])
    marks_copy = pltpu.make_async_copy(marks_v, marks_s, list_sem.at[1])
    lists_copy.start()
    marks_copy.start()

    group = 8

    @pl.loop(0, parts)
    def _(k):
        tile_copy(k).wait()

        @pl.loop(0, per // group)
        def _(s):
            for u in range(group):
                t = k * per + s * group + u
                hi, lo = split2(raw[t])
                halves[t, :TILE] = hi
                halves[t, TILE:] = lo

    lists_copy.wait()
    marks_copy.wait()

    @pl.loop(r + 1, n_row)
    def _(g):
        up_arrival(g).wait_recv()

    @pl.loop(0, n_row)
    def _(g):
        for b in range(BP):
            put_operand(col_x, g * BP + b, col_raw[g, b])

    @pl.when(core == 0)
    def _():
        twin_arrival(chip).wait_recv()
        twin_copy(chip).start()

    @pl.loop(chip + 1, chips)
    def _(q):
        far_arrival(q).wait_recv()
        far_copy(q).start()
        twin_copy(q).start()

    def products(which, operand, forward, between):
        order_at, other_at = 2 * which, 2 * which + 1

        def body(s, total):
            between(s)
            for u in range(unroll):
                k = s * unroll + u
                t = lists_s[order_at, k]
                o = lists_s[other_at, k]
                tile = halves[t]
                if forward:
                    tile = jnp.concatenate([tile[:TILE], tile[TILE:]], axis=1)
                term = lax.dot_general(
                    operand[o], tile, NT if forward else NN, preferred_element_type=F32
                )
                term = term[:width] + term[width:]
                total = total * marks_s[2 * which, k] + term * marks_s[2 * which + 1, k]
                running[k] = total
            return total

        lax.fori_loop(0, steps, body, jnp.zeros((width, TILE), F32))

    def hand_over(s):
        @pl.when(s == steps // 2)
        def _():
            @pl.loop(0, chip)
            def _(q):
                far_arrival(q).wait_recv()
                twin_copy(q).start()

    products(0, col_x, True, hand_over)

    @pl.loop(0, n_col)
    def _(p):
        for b in range(BP):
            k = lists_s[4, p * BP + b]
            row_part[p % 2, p // 2, b] = running[k] * marks_s[4, p * BP + b]

    fold = remote(
        row_part.at[1 - core], from_twin, fold_sem.at[0], fold_sem.at[1], r, twin
    )
    fold.start()

    @pl.when(core == 1)
    def _():
        twin_arrival(chip).wait_recv()

    for d in range(1, chips):
        twin_arrival((chip + d) % chips).wait_recv()

    @pl.loop(0, n_col)
    def _(p):
        for b in range(BP):
            put_operand(row_x, p * BP + b, row_raw[p, b])

    def back_copy(q):
        return remote(
            row_part.at[core, q],
            from_row.at[chip],
            back_send.at[q],
            back_recv.at[chip],
            r,
            q * 2 + core,
        )

    def back_arrival(q):
        return remote(
            from_row.at[q], from_row.at[q], back_send.at[0], back_recv.at[q], r, twin
        )

    def fold_in(s):
        @pl.when(s == jnp.minimum(steps - 1, 5))
        def _():
            fold.wait_recv()

            @pl.loop(1, chips)
            def _(d):
                q = (chip + d) % chips
                row_part[core, q] = row_part[core, q] + from_twin[q]
                back_copy(q).start()

            row_part[core, chip] = row_part[core, chip] + from_twin[chip]

    products(1, row_x, False, fold_in)

    @pl.loop(0, n_row)
    def _(g):
        for b in range(BP):
            k = lists_s[5, g * BP + b]
            col_part[g, b] = running[k] * marks_s[5, g * BP + b]

    def down_copy(g):
        return remote(
            col_part.at[g], from_col.at[r], down_send.at[g], down_recv.at[r], g, c
        )

    def down_arrival(g):
        return remote(
            from_col.at[g], from_col.at[g], down_send.at[0], down_recv.at[g], r, twin
        )

    @pl.loop(r + 1, n_row)
    def _(g):
        down_copy(g).start()

    row_part[core, chip] = row_part[core, chip] + col_part[r]
    for d in range(1, chips):
        q = (chip + d) % chips
        back_arrival(q).wait_recv()
        row_part[core, chip] = row_part[core, chip] + from_row[q]

    @pl.loop(0, r)
    def _(d):
        g = r - 1 - d
        down_arrival(g).wait_recv()
        row_part[core, chip] = row_part[core, chip] + from_col[g]

    for b in range(BP):
        out[:, b * TILE : (b + 1) * TILE] = row_part[core, chip, b]

    @pl.loop(0, r)
    def _(g):
        up_copy(g).wait_send()

    @pl.loop(r + 1, n_row)
    def _(g):
        down_copy(g).wait_send()

    @pl.loop(1, chips)
    def _(d):
        q = (chip + d) % chips
        far_copy(q).wait_send()
        back_copy(q).wait_send()

    for q in range(chips):
        twin_copy(q).wait_send()
    fold.wait_send()


def part_kernel(both, basis, residual):
    half = basis.shape[0]
    basis[...] = both[:half]
    residual[...] = both[half:]


def solution(mesh):
    n_row, n_col = mesh.shape["row"], mesh.shape["col"]
    chips = n_col // 2

    def local(ham_tiles, tile_list, tile_count, basis_block, residual_block):
        slots = ham_tiles.shape[2]
        width = 2 * basis_block.shape[0]
        padded = -(-slots // TILE) * TILE
        unroll = 20 if slots % 20 == 0 else 4
        chunks = 8
        vmem = pl.BlockSpec(memory_space=pltpu.VMEM)
        dma = pltpu.SemaphoreType.DMA
        piece = (BP, width, TILE)
        whole = pl.BlockSpec(memory_space=pltpu.HBM)
        shape = jax.ShapeDtypeStruct(basis_block.shape, F32)
        both = pl.pallas_call(
            functools.partial(kernel, n_row, n_col, unroll, chunks),
            out_shape=jax.ShapeDtypeStruct((width, basis_block.shape[1]), F32),
            in_specs=[
                vmem,
                pl.BlockSpec(memory_space=pltpu.SMEM),
                vmem,
                vmem,
                whole,
            ],
            out_specs=vmem,
            scratch_shapes=[
                pltpu.VMEM((slots, TILE, TILE), F32),
                pltpu.VMEM((slots, 2 * TILE, TILE), BF),
                pltpu.VMEM((slots, width, TILE), F32),
                pltpu.VMEM((n_col,) + piece, F32),
                pltpu.VMEM((n_row,) + piece, F32),
                pltpu.VMEM((n_col * BP, 2 * width, 2 * TILE), BF),
                pltpu.VMEM((n_row * BP, 2 * width, 2 * TILE), BF),
                pltpu.VMEM((2, chips) + piece, F32),
                pltpu.VMEM((chips,) + piece, F32),
                pltpu.VMEM((chips,) + piece, F32),
                pltpu.VMEM((n_row,) + piece, F32),
                pltpu.VMEM((n_row,) + piece, F32),
                pltpu.VMEM((8, padded), I32),
                pltpu.SMEM((8, padded), I32),
                pltpu.VMEM((8, padded), F32),
                pltpu.SMEM((8, padded), F32),
                dma((chunks,)),
                dma((2,)),
                dma((chips,)),
                dma((chips,)),
                dma((chips,)),
                dma((chips,)),
                dma((n_row,)),
                dma((n_row,)),
                dma((2,)),
                dma((chips,)),
                dma((chips,)),
                dma((n_row,)),
                dma((n_row,)),
            ],
            compiler_params=pltpu.CompilerParams(
                collective_id=0,
                has_side_effects=True,
                vmem_limit_bytes=60 * 2**20,
            ),
        )(
            jnp.swapaxes(tile_list, 2, 3),
            tile_count,
            basis_block,
            residual_block,
            ham_tiles,
        )
        return pl.pallas_call(
            part_kernel,
            out_shape=(shape, shape),
            in_specs=[vmem],
            out_specs=(vmem, vmem),
        )(both)

    return jax.shard_map(
        local,
        mesh=mesh,
        in_specs=(
            P("row", "col", None, None, None),
            P("row", "col", None, None),
            P("row", "col"),
            P(None, ("row", "col")),
            P(None, ("row", "col")),
        ),
        out_specs=(P(None, ("row", "col")), P(None, ("row", "col"))),
        check_vma=False,
    )
```

```python
import functools

import jax
import jax.numpy as jnp
from jax import lax
from jax.experimental import pallas as pl
from jax.experimental.pallas import tpu as pltpu
from jax.sharding import PartitionSpec as P

MESH = pl.DeviceIdType.MESH
TILE = 128
BP = 4
BF = jnp.bfloat16
F32 = jnp.float32
I32 = jnp.int32


def split2(value):
    hi = value.astype(BF)
    lo = (value - hi.astype(F32)).astype(BF)
    return hi, lo


def put_operand(dst, index, block):
    rows = block.shape[0]
    hi, lo = split2(block)
    dst[index, :rows, :TILE] = hi
    dst[index, :rows, TILE:] = hi
    dst[index, rows:, :TILE] = lo
    dst[index, rows:, TILE:] = jnp.zeros_like(lo)


def row_of(column, spot):
    return jnp.sum(jnp.where(spot, column, 0), axis=0, keepdims=True)


def column_of(row, spot):
    return jnp.sum(jnp.where(spot, row, 0), axis=1, keepdims=True)


def sorted_lists(key, other, weight2, iota0, iota1, slots):
    tagged = key * 512 + iota0[:, :1]
    tagged_row = row_of(tagged, iota0 == iota1)
    before = (tagged_row < tagged) & (iota1 < slots)
    rank = jnp.sum(jnp.where(before, 1, 0), axis=1, keepdims=True)
    earlier = before & (tagged_row >= key * 512)
    repeats = jnp.minimum(
        jnp.sum(jnp.where(earlier, 1, 0), axis=1, keepdims=True), 1
    )
    place = rank == iota1
    return (
        row_of(iota0[:, :1], place),
        row_of(other, place),
        row_of(repeats, place),
        row_of(weight2, place),
    )


def segment_ends(key, lanes):
    last = jnp.sum(jnp.where(key <= lanes, 1, 0), axis=0, keepdims=True) - 1
    some = jnp.minimum(jnp.sum(jnp.where(key == lanes, 1, 0), axis=0, keepdims=True), 1)
    return jnp.maximum(last, 0), some


def kernel(
    n_row,
    n_col,
    unroll,
    chunks,
    list_ref,
    count_ref,
    basis_ref,
    residual_ref,
    tiles_ref,
    out,
    raw,
    halves,
    turned,
    running,
    row_raw,
    col_raw,
    row_x,
    col_x,
    row_part,
    from_twin,
    from_row,
    col_part,
    from_col,
    lists_v,
    lists_s,
    marks_v,
    marks_s,
    tile_sem,
    list_sem,
    near_sem,
    in_sem,
    side_send,
    side_recv,
    ring_send,
    ring_recv,
    pass_send,
    pass_recv,
    twin_send,
    twin_recv,
    up_send,
    up_recv,
    fold_send,
    fold_recv,
    back_send,
    back_recv,
    down_send,
    down_recv,
):
    slots = halves.shape[0]
    width = row_raw.shape[2]
    half = width // 2
    chips = n_col // 2
    per = slots // chunks
    ring = raw.shape[0]
    blocks = n_col * BP
    r = lax.axis_index("row")
    c = lax.axis_index("col")
    core = c % 2
    chip = c // 2
    twin = chip * 2 + 1 - core
    zs, z, xl = chips // 2, chip // 2, chip % 2
    side = (z * 2 + 1 - xl) * 2 + core

    upper = (n_row - 1 - r) * (BP * blocks) + BP * BP * c + BP * (BP + 1) // 2
    most = (n_row - 1) * (BP * blocks) + BP * BP * (n_col - 1) + BP * (BP + 1) // 2
    bound = jnp.minimum(slots * upper // most + 1, slots)
    steps = (bound + unroll - 1) // unroll
    parts = (steps * unroll + per - 1) // per

    def tile_copy(k):
        return pltpu.make_async_copy(
            tiles_ref.at[0, 0, pl.ds(k * per, per)], raw.at[k % ring], tile_sem.at[k % ring]
        )

    def remote(src, dst, send, recv, row, col):
        return pltpu.make_async_remote_copy(
            src_ref=src,
            dst_ref=dst,
            send_sem=send,
            recv_sem=recv,
            device_id=(row, col),
            device_id_type=MESH,
        )

    @pl.loop(0, jnp.minimum(parts, ring))
    def _(k):
        tile_copy(k).start()

    for b in range(BP):
        columns = slice(b * TILE, (b + 1) * TILE)
        row_raw[c, b, :half] = basis_ref[:, columns]
        row_raw[c, b, half:] = residual_ref[:, columns]
        col_raw[r, b, :half] = basis_ref[:, columns]
        col_raw[r, b, half:] = residual_ref[:, columns]
    for g in range(n_row):

        @pl.when(g < r)
        def _():
            col_raw[g] = jnp.zeros(col_raw.shape[1:], F32)

    barrier = pltpu.get_barrier_semaphore()

    @pl.loop(r + 1, n_row)
    def _(g):
        pl.semaphore_signal(barrier, inc=1, device_id=(g, c), device_id_type=MESH)

    @pl.loop(chip + 1, chips)
    def _(q):
        pl.semaphore_signal(
            barrier, inc=1, device_id=(r, q * 2 + core), device_id_type=MESH
        )

    @pl.when(core == 0)
    def _():
        pl.semaphore_signal(barrier, inc=1, device_id=(r, twin), device_id_type=MESH)

    @pl.when(r + chip + core > 0)
    def _():
        pl.semaphore_wait(barrier, r + chip + core)

    @pl.loop(0, z * 2)
    def _(q):
        pl.semaphore_signal(
            in_sem, inc=1, device_id=(r, q * 2 + core), device_id_type=MESH
        )

    @pl.when(xl == 1)
    def _():
        pl.semaphore_signal(near_sem, inc=1, device_id=(r, side), device_id_type=MESH)

    @pl.when(core == 1)
    def _():
        pl.semaphore_signal(near_sem, inc=1, device_id=(r, twin), device_id_type=MESH)

    def up_copy(g):
        return remote(col_raw.at[r], col_raw.at[r], up_send.at[g], up_recv.at[r], g, c)

    def up_arrival(g):
        return remote(col_raw.at[g], col_raw.at[g], up_send.at[0], up_recv.at[g], r, twin)

    def side_copy():
        return remote(row_raw.at[c], row_raw.at[c], side_send.at[0], side_recv.at[0], r, side)

    def side_arrival():
        return remote(
            row_raw.at[side], row_raw.at[side], side_send.at[0], side_recv.at[0], r, side
        )

    def ring_copy(v):
        to = (v * 2 + xl) * 2 + core
        return remote(row_raw.at[c], row_raw.at[c], ring_send.at[v], ring_recv.at[z], r, to)

    def ring_arrival(v):
        piece = row_raw.at[(v * 2 + xl) * 2 + core]
        return remote(piece, piece, ring_send.at[0], ring_recv.at[v], r, side)

    def pass_copy(v):
        to = (v * 2 + xl) * 2 + core
        return remote(
            row_raw.at[side], row_raw.at[side], pass_send.at[v], pass_recv.at[z], r, to
        )

    def pass_arrival(v):
        piece = row_raw.at[(v * 2 + 1 - xl) * 2 + core]
        return remote(piece, piece, pass_send.at[0], pass_recv.at[v], r, side)

    def twin_copy(q):
        piece = row_raw.at[q * 2 + core]
        return remote(piece, piece, twin_send.at[q], twin_recv.at[q], r, twin)

    def twin_arrival(q):
        piece = row_raw.at[q * 2 + 1 - core]
        return remote(piece, piece, twin_send.at[0], twin_recv.at[q], r, twin)

    @pl.loop(0, r)
    def _(g):
        up_copy(g).start()

    @pl.when(core == 1)
    def _():
        twin_copy(chip).start()

    @pl.when(xl == 1)
    def _():
        side_copy().start()

    @pl.loop(0, z)
    def _(v):
        ring_copy(v).start()

    padded = lists_v.shape[1]
    iota0 = lax.broadcasted_iota(I32, (slots, padded), 0)
    iota1 = lax.broadcasted_iota(I32, (slots, padded), 1)
    listing = jnp.concatenate(
        [list_ref[0, 0], jnp.zeros((2, padded - slots), I32)], axis=1
    )
    local_row = column_of(listing[0:1], iota0 == iota1)
    local_col = column_of(listing[1:2], iota0 == iota1)
    live = iota0[:, :1] < count_ref[0, 0]
    diagonal = (r * (n_col * BP) + local_row) == (
        (local_col // BP) * (n_col * BP) + c * BP + local_col % BP
    )
    weight2 = jnp.where(live, jnp.where(diagonal, 1, 2), 0)
    row_key = jnp.where(live, local_row, blocks)
    col_key = jnp.where(live, local_col, blocks)
    by_row = sorted_lists(row_key, local_col, weight2, iota0, iota1, slots)
    by_col = sorted_lists(col_key, local_row, weight2, iota0, iota1, slots)
    lanes = lax.broadcasted_iota(I32, (slots, TILE), 1)
    row_end, row_some = segment_ends(row_key, lanes)
    col_end, col_some = segment_ends(col_key, lanes)
    for k, (order, other, again, weight) in enumerate((by_row, by_col)):
        lists_v[2 * k : 2 * k + 1] = order
        lists_v[2 * k + 1 : 2 * k + 2] = other
        marks_v[2 * k : 2 * k + 1] = again.astype(F32)
        marks_v[2 * k + 1 : 2 * k + 2] = weight.astype(F32) * 0.5
    lists_v[4:5, :TILE] = row_end
    lists_v[5:6, :TILE] = col_end
    marks_v[4:5, :TILE] = row_some.astype(F32)
    marks_v[5:6, :TILE] = col_some.astype(F32)
    lists_copy = pltpu.make_async_copy(lists_v, lists_s, list_sem.at[0])
    marks_copy = pltpu.make_async_copy(marks_v, marks_s, list_sem.at[1])
    lists_copy.start()
    marks_copy.start()

    group = min(per, 20)

    @pl.loop(0, parts)
    def _(k):
        tile_copy(k).wait()

        @pl.loop(0, per // group)
        def _(s):
            for u in range(group):
                at = s * group + u
                hi, lo = split2(raw[k % ring, at])
                t = k * per + at
                halves[t, :TILE] = hi
                halves[t, TILE:] = lo
                turned[t, :TILE] = hi.T
                turned[t, TILE:] = lo.T

        @pl.when(k + ring < parts)
        def _():
            tile_copy(k + ring).start()

        @pl.when(k == jnp.minimum(parts, 2) - 1)
        def _():
            @pl.when(1 - xl + 1 - core > 0)
            def _():
                pl.semaphore_wait(near_sem, 1 - xl + 1 - core)

            @pl.when(xl == 0)
            def _():
                side_copy().start()

            @pl.when(core == 0)
            def _():
                twin_copy(chip).start()

        @pl.when(k == jnp.minimum(parts, 6) - 1)
        def _():
            @pl.when(zs - 1 - z > 0)
            def _():
                pl.semaphore_wait(in_sem, 2 * (zs - 1 - z))

            @pl.loop(z + 1, zs)
            def _(v):
                ring_copy(v).start()

            side_arrival().wait_recv()

            @pl.loop(1, zs)
            def _(d):
                pass_copy((z + d) % zs).start()

            twin_copy(z * 2 + 1 - xl).start()

    busy = r < 2

    def hand_ring():
        @pl.loop(1, zs)
        def _(d):
            v = (z + d) % zs
            ring_arrival(v).wait_recv()
            twin_copy(v * 2 + xl).start()

    def hand_pass():
        @pl.loop(1, zs)
        def _(d):
            v = (z + d) % zs
            pass_arrival(v).wait_recv()
            twin_copy(v * 2 + 1 - xl).start()

    @pl.when(busy)
    def _():
        hand_ring()

    lists_copy.wait()
    marks_copy.wait()

    @pl.loop(r + 1, n_row)
    def _(g):
        up_arrival(g).wait_recv()

    @pl.loop(0, n_row)
    def _(g):
        for b in range(BP):
            put_operand(col_x, g * BP + b, col_raw[g, b])

    def products(which, operand, tiles, between):
        order_at, other_at = 2 * which, 2 * which + 1

        def body(s, total):
            between(s)
            for u in range(unroll):
                k = s * unroll + u
                t = lists_s[order_at, k]
                o = lists_s[other_at, k]
                term = jnp.dot(operand[o], tiles[t], preferred_element_type=F32)
                term = term[:width] + term[width:]
                total = total * marks_s[2 * which, k] + term * marks_s[2 * which + 1, k]
                running[k] = total
            return total

        lax.fori_loop(0, steps, body, jnp.zeros((width, TILE), F32))

    def hand_over(s):
        @pl.when(busy & (s == steps // 2))
        def _():
            hand_pass()

    products(0, col_x, turned, hand_over)

    @pl.loop(0, n_col)
    def _(p):
        for b in range(BP):
            k = lists_s[4, p * BP + b]
            row_part[p % 2, p // 2, b] = running[k] * marks_s[4, p * BP + b]

    def fold_copy(q):
        return remote(
            row_part.at[1 - core, q], from_twin.at[q], fold_send.at[q], fold_recv.at[q], r, twin
        )

    for d in range(1, chips + 1):
        fold_copy((chip + d) % chips).start()

    def back_copy(q):
        return remote(
            row_part.at[core, q],
            from_row.at[chip],
            back_send.at[q],
            back_recv.at[chip],
            r,
            q * 2 + core,
        )

    def back_arrival(q):
        return remote(
            from_row.at[q], from_row.at[q], back_send.at[0], back_recv.at[q], r, twin
        )

    def add_twin():
        @pl.loop(1, chips)
        def _(d):
            q = (chip + d) % chips
            fold_copy(q).wait_recv()
            row_part[core, q] = row_part[core, q] + from_twin[q]
            back_copy(q).start()

        fold_copy(chip).wait_recv()
        row_part[core, chip] = row_part[core, chip] + from_twin[chip]

    @pl.when(jnp.logical_not(busy))
    def _():
        add_twin()
        hand_ring()
        hand_pass()


    for q in range(chips):
        twin_arrival(q).wait_recv()

    @pl.loop(0, n_col)
    def _(p):
        for b in range(BP):
            put_operand(row_x, p * BP + b, row_raw[p, b])

    def fold_in(s):
        @pl.when(busy & (s == jnp.minimum(steps - 1, 1)))
        def _():
            add_twin()

    products(1, row_x, halves, fold_in)

    @pl.loop(0, n_row)
    def _(g):
        for b in range(BP):
            k = lists_s[5, g * BP + b]
            col_part[g, b] = running[k] * marks_s[5, g * BP + b]

    def down_copy(g):
        return remote(
            col_part.at[g], from_col.at[r], down_send.at[g], down_recv.at[r], g, c
        )

    def down_arrival(g):
        return remote(
            from_col.at[g], from_col.at[g], down_send.at[0], down_recv.at[g], r, twin
        )

    @pl.loop(r + 1, n_row)
    def _(g):
        down_copy(g).start()

    row_part[core, chip] = row_part[core, chip] + col_part[r]
    for d in range(1, chips):
        q = (chip + d) % chips
        back_arrival(q).wait_recv()
        row_part[core, chip] = row_part[core, chip] + from_row[q]

    @pl.loop(0, r)
    def _(d):
        g = r - 1 - d
        down_arrival(g).wait_recv()
        row_part[core, chip] = row_part[core, chip] + from_col[g]

    for b in range(BP):
        out[:, b * TILE : (b + 1) * TILE] = row_part[core, chip, b]

    @pl.loop(0, r)
    def _(g):
        up_copy(g).wait_send()

    @pl.loop(r + 1, n_row)
    def _(g):
        down_copy(g).wait_send()

    @pl.loop(1, chips)
    def _(d):
        q = (chip + d) % chips
        back_copy(q).wait_send()

    side_copy().wait_send()

    @pl.loop(1, zs)
    def _(d):
        ring_copy((z + d) % zs).wait_send()
        pass_copy((z + d) % zs).wait_send()

    for q in range(chips):
        twin_copy(q).wait_send()
        fold_copy(q).wait_send()


def part_kernel(both, basis, residual):
    half = basis.shape[0]
    basis[...] = both[:half]
    residual[...] = both[half:]


def solution(mesh):
    n_row, n_col = mesh.shape["row"], mesh.shape["col"]
    chips = n_col // 2

    def local(ham_tiles, tile_list, tile_count, basis_block, residual_block):
        slots = ham_tiles.shape[2]
        width = 2 * basis_block.shape[0]
        padded = -(-slots // TILE) * TILE
        unroll = 32 if slots % 32 == 0 else 20
        chunks = 16
        ring = 4
        vmem = pl.BlockSpec(memory_space=pltpu.VMEM)
        dma = pltpu.SemaphoreType.DMA
        piece = (BP, width, TILE)
        whole = pl.BlockSpec(memory_space=pltpu.HBM)
        shape = jax.ShapeDtypeStruct(basis_block.shape, F32)
        both = pl.pallas_call(
            functools.partial(kernel, n_row, n_col, unroll, chunks),
            out_shape=jax.ShapeDtypeStruct((width, basis_block.shape[1]), F32),
            in_specs=[
                vmem,
                pl.BlockSpec(memory_space=pltpu.SMEM),
                vmem,
                vmem,
                whole,
            ],
            out_specs=vmem,
            scratch_shapes=[
                pltpu.VMEM((ring, slots // chunks, TILE, TILE), F32),
                pltpu.VMEM((slots, 2 * TILE, TILE), BF),
                pltpu.VMEM((slots, 2 * TILE, TILE), BF),
                pltpu.VMEM((slots, width, TILE), F32),
                pltpu.VMEM((n_col,) + piece, F32),
                pltpu.VMEM((n_row,) + piece, F32),
                pltpu.VMEM((n_col * BP, 2 * width, 2 * TILE), BF),
                pltpu.VMEM((n_row * BP, 2 * width, 2 * TILE), BF),
                pltpu.VMEM((2, chips) + piece, F32),
                pltpu.VMEM((chips,) + piece, F32),
                pltpu.VMEM((chips,) + piece, F32),
                pltpu.VMEM((n_row,) + piece, F32),
                pltpu.VMEM((n_row,) + piece, F32),
                pltpu.VMEM((8, padded), I32),
                pltpu.SMEM((8, padded), I32),
                pltpu.VMEM((8, padded), F32),
                pltpu.SMEM((8, padded), F32),
                dma((ring,)),
                dma((2,)),
                pltpu.SemaphoreType.REGULAR,
                pltpu.SemaphoreType.REGULAR,
                dma((1,)),
                dma((1,)),
                dma((chips // 2,)),
                dma((chips // 2,)),
                dma((chips // 2,)),
                dma((chips // 2,)),
                dma((chips,)),
                dma((chips,)),
                dma((n_row,)),
                dma((n_row,)),
                dma((chips,)),
                dma((chips,)),
                dma((chips,)),
                dma((chips,)),
                dma((n_row,)),
                dma((n_row,)),
            ],
            compiler_params=pltpu.CompilerParams(
                collective_id=0,
                has_side_effects=True,
                vmem_limit_bytes=60 * 2**20,
            ),
        )(
            jnp.swapaxes(tile_list, 2, 3),
            tile_count,
            basis_block,
            residual_block,
            ham_tiles,
        )
        return pl.pallas_call(
            part_kernel,
            out_shape=(shape, shape),
            in_specs=[vmem],
            out_specs=(vmem, vmem),
        )(both)

    return jax.shard_map(
        local,
        mesh=mesh,
        in_specs=(
            P("row", "col", None, None, None),
            P("row", "col", None, None),
            P("row", "col"),
            P(None, ("row", "col")),
            P(None, ("row", "col")),
        ),
        out_specs=(P(None, ("row", "col")), P(None, ("row", "col"))),
        check_vma=False,
    )
```

```python
import functools

import jax
import jax.numpy as jnp
from jax import lax
from jax.experimental import pallas as pl
from jax.experimental.pallas import tpu as pltpu
from jax.sharding import PartitionSpec as P

MESH = pl.DeviceIdType.MESH
TILE = 128
BP = 4
BF = jnp.bfloat16
F32 = jnp.float32
I32 = jnp.int32


def split2(value):
    hi = value.astype(BF)
    lo = (value - hi.astype(F32)).astype(BF)
    return hi, lo


def put_operand(dst, index, block):
    rows = block.shape[0]
    hi, lo = split2(block)
    dst[index, :rows, :TILE] = hi
    dst[index, :rows, TILE:] = hi
    dst[index, rows:, :TILE] = lo
    dst[index, rows:, TILE:] = jnp.zeros_like(lo)


def row_of(column, spot):
    return jnp.sum(jnp.where(spot, column, 0), axis=0, keepdims=True)


def column_of(row, spot):
    return jnp.sum(jnp.where(spot, row, 0), axis=1, keepdims=True)


def sorted_lists(key, other, weight2, iota0, iota1, slots):
    tagged = key * 512 + iota0[:, :1]
    tagged_row = row_of(tagged, iota0 == iota1)
    before = (tagged_row < tagged) & (iota1 < slots)
    rank = jnp.sum(jnp.where(before, 1, 0), axis=1, keepdims=True)
    earlier = before & (tagged_row >= key * 512)
    repeats = jnp.minimum(
        jnp.sum(jnp.where(earlier, 1, 0), axis=1, keepdims=True), 1
    )
    place = rank == iota1
    return (
        row_of(iota0[:, :1], place),
        row_of(other, place),
        row_of(repeats, place),
        row_of(weight2, place),
    )


def segment_ends(key, lanes):
    last = jnp.sum(jnp.where(key <= lanes, 1, 0), axis=0, keepdims=True) - 1
    some = jnp.minimum(jnp.sum(jnp.where(key == lanes, 1, 0), axis=0, keepdims=True), 1)
    return jnp.maximum(last, 0), some


def kernel(
    n_row,
    n_col,
    unroll,
    chunks,
    list_ref,
    count_ref,
    basis_ref,
    residual_ref,
    tiles_ref,
    out,
    raw,
    halves,
    turned,
    running,
    row_raw,
    col_raw,
    row_x,
    col_x,
    row_part,
    from_twin,
    from_row,
    col_part,
    from_col,
    lists_v,
    lists_s,
    marks_v,
    marks_s,
    tile_sem,
    list_sem,
    near_sem,
    in_sem,
    side_send,
    side_recv,
    ring_send,
    ring_recv,
    pass_send,
    pass_recv,
    twin_send,
    twin_recv,
    up_send,
    up_recv,
    fold_send,
    fold_recv,
    back_send,
    back_recv,
    down_send,
    down_recv,
):
    slots = halves.shape[0]
    width = row_raw.shape[2]
    half = width // 2
    chips = n_col // 2
    per = slots // chunks
    ring = raw.shape[0]
    blocks = n_col * BP
    r = lax.axis_index("row")
    c = lax.axis_index("col")
    core = c % 2
    chip = c // 2
    twin = chip * 2 + 1 - core
    zs, z, xl = chips // 2, chip // 2, chip % 2
    side = (z * 2 + 1 - xl) * 2 + core

    upper = (n_row - 1 - r) * (BP * blocks) + BP * BP * c + BP * (BP + 1) // 2
    most = (n_row - 1) * (BP * blocks) + BP * BP * (n_col - 1) + BP * (BP + 1) // 2
    bound = jnp.minimum(slots * upper // most + 1, slots)
    steps = (bound + unroll - 1) // unroll
    parts = (steps * unroll + per - 1) // per

    def tile_copy(k):
        return pltpu.make_async_copy(
            tiles_ref.at[0, 0, pl.ds(k * per, per)], raw.at[k % ring], tile_sem.at[k % ring]
        )

    def remote(src, dst, send, recv, row, col):
        return pltpu.make_async_remote_copy(
            src_ref=src,
            dst_ref=dst,
            send_sem=send,
            recv_sem=recv,
            device_id=(row, col),
            device_id_type=MESH,
        )

    @pl.loop(0, jnp.minimum(parts, ring))
    def _(k):
        tile_copy(k).start()

    for b in range(BP):
        columns = slice(b * TILE, (b + 1) * TILE)
        row_raw[c, b, :half] = basis_ref[:, columns]
        row_raw[c, b, half:] = residual_ref[:, columns]
        col_raw[r, b, :half] = basis_ref[:, columns]
        col_raw[r, b, half:] = residual_ref[:, columns]
    for g in range(n_row):

        @pl.when(g < r)
        def _():
            col_raw[g] = jnp.zeros(col_raw.shape[1:], F32)

    barrier = pltpu.get_barrier_semaphore()

    @pl.loop(r + 1, n_row)
    def _(g):
        pl.semaphore_signal(barrier, inc=1, device_id=(g, c), device_id_type=MESH)

    @pl.loop(chip + 1, chips)
    def _(q):
        pl.semaphore_signal(
            barrier, inc=1, device_id=(r, q * 2 + core), device_id_type=MESH
        )

    @pl.when(core == 0)
    def _():
        pl.semaphore_signal(barrier, inc=1, device_id=(r, twin), device_id_type=MESH)

    @pl.when(r + chip + core > 0)
    def _():
        pl.semaphore_wait(barrier, r + chip + core)

    @pl.loop(0, z * 2)
    def _(q):
        pl.semaphore_signal(
            in_sem, inc=1, device_id=(r, q * 2 + core), device_id_type=MESH
        )

    @pl.when(xl == 1)
    def _():
        pl.semaphore_signal(near_sem, inc=1, device_id=(r, side), device_id_type=MESH)

    @pl.when(core == 1)
    def _():
        pl.semaphore_signal(near_sem, inc=1, device_id=(r, twin), device_id_type=MESH)

    def up_copy(g):
        return remote(col_raw.at[r], col_raw.at[r], up_send.at[g], up_recv.at[r], g, c)

    def up_arrival(g):
        return remote(col_raw.at[g], col_raw.at[g], up_send.at[0], up_recv.at[g], r, twin)

    def side_copy():
        return remote(row_raw.at[c], row_raw.at[c], side_send.at[0], side_recv.at[0], r, side)

    def side_arrival():
        return remote(
            row_raw.at[side], row_raw.at[side], side_send.at[0], side_recv.at[0], r, side
        )

    def ring_copy(v):
        to = (v * 2 + xl) * 2 + core
        return remote(row_raw.at[c], row_raw.at[c], ring_send.at[v], ring_recv.at[z], r, to)

    def ring_arrival(v):
        piece = row_raw.at[(v * 2 + xl) * 2 + core]
        return remote(piece, piece, ring_send.at[0], ring_recv.at[v], r, side)

    def pass_copy(v):
        to = (v * 2 + xl) * 2 + core
        return remote(
            row_raw.at[side], row_raw.at[side], pass_send.at[v], pass_recv.at[z], r, to
        )

    def pass_arrival(v):
        piece = row_raw.at[(v * 2 + 1 - xl) * 2 + core]
        return remote(piece, piece, pass_send.at[0], pass_recv.at[v], r, side)

    def twin_copy(q):
        piece = row_raw.at[q * 2 + core]
        return remote(piece, piece, twin_send.at[q], twin_recv.at[q], r, twin)

    def twin_arrival(q):
        piece = row_raw.at[q * 2 + 1 - core]
        return remote(piece, piece, twin_send.at[0], twin_recv.at[q], r, twin)

    @pl.loop(0, r)
    def _(g):
        up_copy(g).start()

    @pl.when(core == 1)
    def _():
        twin_copy(chip).start()

    @pl.when(xl == 1)
    def _():
        side_copy().start()

    @pl.loop(0, z)
    def _(v):
        ring_copy(v).start()

    padded = lists_v.shape[1]
    iota0 = lax.broadcasted_iota(I32, (slots, padded), 0)
    iota1 = lax.broadcasted_iota(I32, (slots, padded), 1)
    listing = jnp.concatenate(
        [list_ref[0, 0], jnp.zeros((2, padded - slots), I32)], axis=1
    )
    local_row = column_of(listing[0:1], iota0 == iota1)
    local_col = column_of(listing[1:2], iota0 == iota1)
    live = iota0[:, :1] < count_ref[0, 0]
    diagonal = (r * (n_col * BP) + local_row) == (
        (local_col // BP) * (n_col * BP) + c * BP + local_col % BP
    )
    weight2 = jnp.where(live, jnp.where(diagonal, 1, 2), 0)
    row_key = jnp.where(live, local_row, blocks)
    col_key = jnp.where(live, local_col, blocks)
    by_row = sorted_lists(row_key, local_col, weight2, iota0, iota1, slots)
    by_col = sorted_lists(col_key, local_row, weight2, iota0, iota1, slots)
    lanes = lax.broadcasted_iota(I32, (slots, TILE), 1)
    row_end, row_some = segment_ends(row_key, lanes)
    col_end, col_some = segment_ends(col_key, lanes)
    for k, (order, other, again, weight) in enumerate((by_row, by_col)):
        lists_v[2 * k : 2 * k + 1] = order
        lists_v[2 * k + 1 : 2 * k + 2] = other
        marks_v[2 * k : 2 * k + 1] = again.astype(F32)
        marks_v[2 * k + 1 : 2 * k + 2] = weight.astype(F32) * 0.5
    lists_v[4:5, :TILE] = row_end
    lists_v[5:6, :TILE] = col_end
    marks_v[4:5, :TILE] = row_some.astype(F32)
    marks_v[5:6, :TILE] = col_some.astype(F32)
    lists_copy = pltpu.make_async_copy(lists_v, lists_s, list_sem.at[0])
    marks_copy = pltpu.make_async_copy(marks_v, marks_s, list_sem.at[1])
    lists_copy.start()
    marks_copy.start()

    group = min(per, 20)

    @pl.loop(0, parts)
    def _(k):
        tile_copy(k).wait()

        @pl.loop(0, per // group)
        def _(s):
            for u in range(group):
                at = s * group + u
                hi, lo = split2(raw[k % ring, at])
                t = k * per + at
                halves[t, :TILE] = hi
                halves[t, TILE:] = lo
                turned[t, :TILE] = hi.T
                turned[t, TILE:] = lo.T

        @pl.when(k + ring < parts)
        def _():
            tile_copy(k + ring).start()

        @pl.when(k == jnp.minimum(parts, 2) - 1)
        def _():
            @pl.when(1 - xl + 1 - core > 0)
            def _():
                pl.semaphore_wait(near_sem, 1 - xl + 1 - core)

            @pl.when(xl == 0)
            def _():
                side_copy().start()

            @pl.when(core == 0)
            def _():
                twin_copy(chip).start()

        @pl.when(k == jnp.minimum(parts, 6) - 1)
        def _():
            @pl.when(zs - 1 - z > 0)
            def _():
                pl.semaphore_wait(in_sem, 2 * (zs - 1 - z))

            @pl.loop(z + 1, zs)
            def _(v):
                ring_copy(v).start()

            side_arrival().wait_recv()

            @pl.loop(1, zs)
            def _(d):
                pass_copy((z + d) % zs).start()

            twin_copy(z * 2 + 1 - xl).start()

    busy = r < 2

    def hand_ring():
        @pl.loop(1, zs)
        def _(d):
            v = (z + d) % zs
            ring_arrival(v).wait_recv()
            twin_copy(v * 2 + xl).start()

    def hand_pass():
        @pl.loop(1, zs)
        def _(d):
            v = (z + d) % zs
            pass_arrival(v).wait_recv()
            twin_copy(v * 2 + 1 - xl).start()

    @pl.when(busy)
    def _():
        hand_ring()

    lists_copy.wait()
    marks_copy.wait()

    @pl.loop(r + 1, n_row)
    def _(g):
        up_arrival(g).wait_recv()

    @pl.loop(0, n_row)
    def _(g):
        for b in range(BP):
            put_operand(col_x, g * BP + b, col_raw[g, b])

    def products(which, operand, tiles, between):
        order_at, other_at = 2 * which, 2 * which + 1

        def body(s, total):
            between(s)
            for u in range(unroll):
                k = s * unroll + u
                t = lists_s[order_at, k]
                o = lists_s[other_at, k]
                term = jnp.dot(operand[o], tiles[t], preferred_element_type=F32)
                term = term[:width] + term[width:]
                total = total * marks_s[2 * which, k] + term * marks_s[2 * which + 1, k]
                running[k] = total
            return total

        lax.fori_loop(0, steps, body, jnp.zeros((width, TILE), F32))

    def hand_over(s):
        @pl.when(busy & (s == steps // 2))
        def _():
            hand_pass()

    products(0, col_x, turned, hand_over)

    @pl.loop(0, n_col)
    def _(p):
        for b in range(BP):
            k = lists_s[4, p * BP + b]
            row_part[p % 2, p // 2, b] = running[k] * marks_s[4, p * BP + b]

    def fold_copy(q):
        return remote(
            row_part.at[1 - core, q], from_twin.at[q], fold_send.at[q], fold_recv.at[q], r, twin
        )

    for d in range(1, chips + 1):
        fold_copy((chip + d) % chips).start()

    def back_copy(q):
        return remote(
            row_part.at[core, q],
            from_row.at[chip],
            back_send.at[q],
            back_recv.at[chip],
            r,
            q * 2 + core,
        )

    def back_arrival(q):
        return remote(
            from_row.at[q], from_row.at[q], back_send.at[0], back_recv.at[q], r, twin
        )

    def add_twin():
        @pl.loop(1, chips)
        def _(d):
            q = (chip + d) % chips
            fold_copy(q).wait_recv()
            row_part[core, q] = row_part[core, q] + from_twin[q]
            back_copy(q).start()

        fold_copy(chip).wait_recv()
        row_part[core, chip] = row_part[core, chip] + from_twin[chip]

    @pl.when(jnp.logical_not(busy))
    def _():
        add_twin()
        hand_ring()
        hand_pass()


    for q in range(chips):
        twin_arrival(q).wait_recv()

    @pl.loop(0, n_col)
    def _(p):
        for b in range(BP):
            put_operand(row_x, p * BP + b, row_raw[p, b])

    def fold_in(s):
        @pl.when(busy & (s == jnp.minimum(steps - 1, 1)))
        def _():
            add_twin()

    products(1, row_x, halves, fold_in)

    @pl.loop(0, n_row)
    def _(g):
        for b in range(BP):
            k = lists_s[5, g * BP + b]
            col_part[g, b] = running[k] * marks_s[5, g * BP + b]

    def down_copy(g):
        return remote(
            col_part.at[g], from_col.at[r], down_send.at[g], down_recv.at[r], g, c
        )

    def down_arrival(g):
        return remote(
            from_col.at[g], from_col.at[g], down_send.at[0], down_recv.at[g], r, twin
        )

    @pl.loop(0, n_row - 1 - r)
    def _(d):
        down_copy(n_row - 1 - d).start()

    row_part[core, chip] = row_part[core, chip] + col_part[r]
    for d in range(1, chips):
        q = (chip + d) % chips
        back_arrival(q).wait_recv()
        row_part[core, chip] = row_part[core, chip] + from_row[q]

    @pl.loop(0, r)
    def _(d):
        g = r - 1 - d
        down_arrival(g).wait_recv()
        row_part[core, chip] = row_part[core, chip] + from_col[g]

    for b in range(BP):
        out[:, b * TILE : (b + 1) * TILE] = row_part[core, chip, b]

    @pl.loop(0, r)
    def _(g):
        up_copy(g).wait_send()

    @pl.loop(r + 1, n_row)
    def _(g):
        down_copy(g).wait_send()

    @pl.loop(1, chips)
    def _(d):
        q = (chip + d) % chips
        back_copy(q).wait_send()

    side_copy().wait_send()

    @pl.loop(1, zs)
    def _(d):
        ring_copy((z + d) % zs).wait_send()
        pass_copy((z + d) % zs).wait_send()

    for q in range(chips):
        twin_copy(q).wait_send()
        fold_copy(q).wait_send()


def part_kernel(both, basis, residual):
    half = basis.shape[0]
    basis[...] = both[:half]
    residual[...] = both[half:]


def solution(mesh):
    n_row, n_col = mesh.shape["row"], mesh.shape["col"]
    chips = n_col // 2

    def local(ham_tiles, tile_list, tile_count, basis_block, residual_block):
        slots = ham_tiles.shape[2]
        width = 2 * basis_block.shape[0]
        padded = -(-slots // TILE) * TILE
        unroll = 80
        chunks = 16
        ring = 4
        vmem = pl.BlockSpec(memory_space=pltpu.VMEM)
        dma = pltpu.SemaphoreType.DMA
        piece = (BP, width, TILE)
        whole = pl.BlockSpec(memory_space=pltpu.HBM)
        shape = jax.ShapeDtypeStruct(basis_block.shape, F32)
        both = pl.pallas_call(
            functools.partial(kernel, n_row, n_col, unroll, chunks),
            out_shape=jax.ShapeDtypeStruct((width, basis_block.shape[1]), F32),
            in_specs=[
                vmem,
                pl.BlockSpec(memory_space=pltpu.SMEM),
                vmem,
                vmem,
                whole,
            ],
            out_specs=vmem,
            scratch_shapes=[
                pltpu.VMEM((ring, slots // chunks, TILE, TILE), F32),
                pltpu.VMEM((slots, 2 * TILE, TILE), BF),
                pltpu.VMEM((slots, 2 * TILE, TILE), BF),
                pltpu.VMEM((slots, width, TILE), F32),
                pltpu.VMEM((n_col,) + piece, F32),
                pltpu.VMEM((n_row,) + piece, F32),
                pltpu.VMEM((n_col * BP, 2 * width, 2 * TILE), BF),
                pltpu.VMEM((n_row * BP, 2 * width, 2 * TILE), BF),
                pltpu.VMEM((2, chips) + piece, F32),
                pltpu.VMEM((chips,) + piece, F32),
                pltpu.VMEM((chips,) + piece, F32),
                pltpu.VMEM((n_row,) + piece, F32),
                pltpu.VMEM((n_row,) + piece, F32),
                pltpu.VMEM((8, padded), I32),
                pltpu.SMEM((8, padded), I32),
                pltpu.VMEM((8, padded), F32),
                pltpu.SMEM((8, padded), F32),
                dma((ring,)),
                dma((2,)),
                pltpu.SemaphoreType.REGULAR,
                pltpu.SemaphoreType.REGULAR,
                dma((1,)),
                dma((1,)),
                dma((chips // 2,)),
                dma((chips // 2,)),
                dma((chips // 2,)),
                dma((chips // 2,)),
                dma((chips,)),
                dma((chips,)),
                dma((n_row,)),
                dma((n_row,)),
                dma((chips,)),
                dma((chips,)),
                dma((chips,)),
                dma((chips,)),
                dma((n_row,)),
                dma((n_row,)),
            ],
            compiler_params=pltpu.CompilerParams(
                collective_id=0,
                has_side_effects=True,
                vmem_limit_bytes=60 * 2**20,
            ),
        )(
            jnp.swapaxes(tile_list, 2, 3),
            tile_count,
            basis_block,
            residual_block,
            ham_tiles,
        )
        return pl.pallas_call(
            part_kernel,
            out_shape=(shape, shape),
            in_specs=[vmem],
            out_specs=(vmem, vmem),
        )(both)

    return jax.shard_map(
        local,
        mesh=mesh,
        in_specs=(
            P("row", "col", None, None, None),
            P("row", "col", None, None),
            P("row", "col"),
            P(None, ("row", "col")),
            P(None, ("row", "col")),
        ),
        out_specs=(P(None, ("row", "col")), P(None, ("row", "col"))),
        check_vma=False,
    )
```

```python
import functools

import jax
import jax.numpy as jnp
from jax import lax
from jax.experimental import pallas as pl
from jax.experimental.pallas import tpu as pltpu
from jax.sharding import PartitionSpec as P

MESH = pl.DeviceIdType.MESH
TILE = 128
BP = 4
BF = jnp.bfloat16
F32 = jnp.float32
I32 = jnp.int32


def split2(value):
    hi = value.astype(BF)
    lo = (value - hi.astype(F32)).astype(BF)
    return hi, lo


def put_operand(dst, index, block):
    rows = block.shape[0]
    hi, lo = split2(block)
    dst[index, :rows, :TILE] = hi
    dst[index, :rows, TILE:] = hi
    dst[index, rows:, :TILE] = lo
    dst[index, rows:, TILE:] = jnp.zeros_like(lo)


def row_of(column, spot):
    return jnp.sum(jnp.where(spot, column, 0), axis=0, keepdims=True)


def column_of(row, spot):
    return jnp.sum(jnp.where(spot, row, 0), axis=1, keepdims=True)


def sorted_lists(key, other, weight2, iota0, iota1, slots):
    tagged = key * 512 + iota0[:, :1]
    tagged_row = row_of(tagged, iota0 == iota1)
    before = (tagged_row < tagged) & (iota1 < slots)
    rank = jnp.sum(jnp.where(before, 1, 0), axis=1, keepdims=True)
    earlier = before & (tagged_row >= key * 512)
    repeats = jnp.minimum(
        jnp.sum(jnp.where(earlier, 1, 0), axis=1, keepdims=True), 1
    )
    place = rank == iota1
    return (
        row_of(iota0[:, :1], place),
        row_of(other, place),
        row_of(repeats, place),
        row_of(weight2, place),
    )


def segment_ends(key, lanes):
    last = jnp.sum(jnp.where(key <= lanes, 1, 0), axis=0, keepdims=True) - 1
    some = jnp.minimum(jnp.sum(jnp.where(key == lanes, 1, 0), axis=0, keepdims=True), 1)
    return jnp.maximum(last, 0), some


def kernel(
    n_row,
    n_col,
    unroll,
    chunks,
    list_ref,
    count_ref,
    basis_ref,
    residual_ref,
    tiles_ref,
    out,
    raw,
    halves,
    turned,
    running,
    row_raw,
    col_raw,
    row_x,
    col_x,
    row_part,
    from_twin,
    from_row,
    col_part,
    from_col,
    lists_v,
    lists_s,
    marks_v,
    marks_s,
    list_v,
    own_sem,
    tile_sem,
    list_sem,
    near_sem,
    in_sem,
    side_send,
    side_recv,
    ring_send,
    ring_recv,
    pass_send,
    pass_recv,
    twin_send,
    twin_recv,
    up_send,
    up_recv,
    fold_send,
    fold_recv,
    back_send,
    back_recv,
    down_send,
    down_recv,
):
    slots = halves.shape[0]
    width = row_raw.shape[2]
    half = width // 2
    chips = n_col // 2
    per = slots // chunks
    ring = raw.shape[0]
    blocks = n_col * BP
    r = lax.axis_index("row")
    c = lax.axis_index("col")
    core = c % 2
    chip = c // 2
    twin = chip * 2 + 1 - core
    zs, z, xl = chips // 2, chip // 2, chip % 2
    side = (z * 2 + 1 - xl) * 2 + core

    upper = (n_row - 1 - r) * (BP * blocks) + BP * BP * c + BP * (BP + 1) // 2
    most = (n_row - 1) * (BP * blocks) + BP * BP * (n_col - 1) + BP * (BP + 1) // 2
    bound = jnp.minimum(slots * upper // most + 1, slots)
    steps = (bound + unroll - 1) // unroll
    parts = (steps * unroll + per - 1) // per

    def tile_copy(k):
        return pltpu.make_async_copy(
            tiles_ref.at[0, 0, pl.ds(k * per, per)], raw.at[k % ring], tile_sem.at[k % ring]
        )

    def remote(src, dst, send, recv, row, col):
        return pltpu.make_async_remote_copy(
            src_ref=src,
            dst_ref=dst,
            send_sem=send,
            recv_sem=recv,
            device_id=(row, col),
            device_id_type=MESH,
        )

    own = []
    for b in range(BP):
        columns = pl.ds(b * TILE, TILE)
        for k, ref in enumerate((basis_ref, residual_ref)):
            own.append(
                pltpu.make_async_copy(
                    ref.at[:, columns],
                    row_raw.at[c, b, pl.ds(k * half, half)],
                    own_sem.at[2 * b + k],
                )
            )
    own.append(pltpu.make_async_copy(list_ref, list_v, own_sem.at[2 * BP]))
    for copy in own:
        copy.start()

    @pl.loop(0, jnp.minimum(parts, ring))
    def _(k):
        tile_copy(k).start()

    for g in range(n_row):

        @pl.when(g < r)
        def _():
            col_raw[g] = jnp.zeros(col_raw.shape[1:], F32)

    barrier = pltpu.get_barrier_semaphore()

    @pl.loop(r + 1, n_row)
    def _(g):
        pl.semaphore_signal(barrier, inc=1, device_id=(g, c), device_id_type=MESH)

    @pl.loop(chip + 1, chips)
    def _(q):
        pl.semaphore_signal(
            barrier, inc=1, device_id=(r, q * 2 + core), device_id_type=MESH
        )

    @pl.when(core == 0)
    def _():
        pl.semaphore_signal(barrier, inc=1, device_id=(r, twin), device_id_type=MESH)

    @pl.when(r + chip + core > 0)
    def _():
        pl.semaphore_wait(barrier, r + chip + core)

    for copy in own[:-1]:
        copy.wait()

    @pl.loop(0, z * 2)
    def _(q):
        pl.semaphore_signal(
            in_sem, inc=1, device_id=(r, q * 2 + core), device_id_type=MESH
        )

    @pl.when(xl == 1)
    def _():
        pl.semaphore_signal(near_sem, inc=1, device_id=(r, side), device_id_type=MESH)

    @pl.when(core == 1)
    def _():
        pl.semaphore_signal(near_sem, inc=1, device_id=(r, twin), device_id_type=MESH)

    def up_copy(g):
        return remote(row_raw.at[c], col_raw.at[r], up_send.at[g], up_recv.at[r], g, c)

    def up_arrival(g):
        return remote(col_raw.at[g], col_raw.at[g], up_send.at[0], up_recv.at[g], r, twin)

    def side_copy():
        return remote(row_raw.at[c], row_raw.at[c], side_send.at[0], side_recv.at[0], r, side)

    def side_arrival():
        return remote(
            row_raw.at[side], row_raw.at[side], side_send.at[0], side_recv.at[0], r, side
        )

    def ring_copy(v):
        to = (v * 2 + xl) * 2 + core
        return remote(row_raw.at[c], row_raw.at[c], ring_send.at[v], ring_recv.at[z], r, to)

    def ring_arrival(v):
        piece = row_raw.at[(v * 2 + xl) * 2 + core]
        return remote(piece, piece, ring_send.at[0], ring_recv.at[v], r, side)

    def pass_copy(v):
        to = (v * 2 + xl) * 2 + core
        return remote(
            row_raw.at[side], row_raw.at[side], pass_send.at[v], pass_recv.at[z], r, to
        )

    def pass_arrival(v):
        piece = row_raw.at[(v * 2 + 1 - xl) * 2 + core]
        return remote(piece, piece, pass_send.at[0], pass_recv.at[v], r, side)

    def twin_copy(q):
        piece = row_raw.at[q * 2 + core]
        return remote(piece, piece, twin_send.at[q], twin_recv.at[q], r, twin)

    def twin_arrival(q):
        piece = row_raw.at[q * 2 + 1 - core]
        return remote(piece, piece, twin_send.at[0], twin_recv.at[q], r, twin)

    @pl.loop(0, r)
    def _(g):
        up_copy(g).start()

    @pl.when(core == 1)
    def _():
        twin_copy(chip).start()

    @pl.when(xl == 1)
    def _():
        side_copy().start()

    @pl.loop(0, z)
    def _(v):
        ring_copy(v).start()

    col_raw[r] = row_raw[c]
    own[-1].wait()

    padded = lists_v.shape[1]
    iota0 = lax.broadcasted_iota(I32, (slots, padded), 0)
    iota1 = lax.broadcasted_iota(I32, (slots, padded), 1)
    listing = jnp.concatenate(
        [list_v[0, 0], jnp.zeros((2, padded - slots), I32)], axis=1
    )
    local_row = column_of(listing[0:1], iota0 == iota1)
    local_col = column_of(listing[1:2], iota0 == iota1)
    live = iota0[:, :1] < count_ref[0, 0]
    diagonal = (r * (n_col * BP) + local_row) == (
        (local_col // BP) * (n_col * BP) + c * BP + local_col % BP
    )
    weight2 = jnp.where(live, jnp.where(diagonal, 1, 2), 0)
    row_key = jnp.where(live, local_row, blocks)
    col_key = jnp.where(live, local_col, blocks)
    by_row = sorted_lists(row_key, local_col, weight2, iota0, iota1, slots)
    by_col = sorted_lists(col_key, local_row, weight2, iota0, iota1, slots)
    lanes = lax.broadcasted_iota(I32, (slots, TILE), 1)
    row_end, row_some = segment_ends(row_key, lanes)
    col_end, col_some = segment_ends(col_key, lanes)
    for k, (order, other, again, weight) in enumerate((by_row, by_col)):
        lists_v[2 * k : 2 * k + 1] = order
        lists_v[2 * k + 1 : 2 * k + 2] = other
        marks_v[2 * k : 2 * k + 1] = again.astype(F32)
        marks_v[2 * k + 1 : 2 * k + 2] = weight.astype(F32) * 0.5
    lists_v[4:5, :TILE] = row_end
    lists_v[5:6, :TILE] = col_end
    marks_v[4:5, :TILE] = row_some.astype(F32)
    marks_v[5:6, :TILE] = col_some.astype(F32)
    lists_copy = pltpu.make_async_copy(lists_v, lists_s, list_sem.at[0])
    marks_copy = pltpu.make_async_copy(marks_v, marks_s, list_sem.at[1])
    lists_copy.start()
    marks_copy.start()

    group = min(per, 20)

    @pl.loop(0, parts)
    def _(k):
        tile_copy(k).wait()

        @pl.loop(0, per // group)
        def _(s):
            for u in range(group):
                at = s * group + u
                hi, lo = split2(raw[k % ring, at])
                t = k * per + at
                halves[t, :TILE] = hi
                halves[t, TILE:] = lo
                turned[t, :TILE] = hi.T
                turned[t, TILE:] = lo.T

        @pl.when(k + ring < parts)
        def _():
            tile_copy(k + ring).start()

        @pl.when(k == jnp.minimum(parts, 2) - 1)
        def _():
            @pl.when(1 - xl + 1 - core > 0)
            def _():
                pl.semaphore_wait(near_sem, 1 - xl + 1 - core)

            @pl.when(xl == 0)
            def _():
                side_copy().start()

            @pl.when(core == 0)
            def _():
                twin_copy(chip).start()

        @pl.when(k == jnp.minimum(parts, 6) - 1)
        def _():
            @pl.when(zs - 1 - z > 0)
            def _():
                pl.semaphore_wait(in_sem, 2 * (zs - 1 - z))

            @pl.loop(z + 1, zs)
            def _(v):
                ring_copy(v).start()

            side_arrival().wait_recv()

            @pl.loop(1, zs)
            def _(d):
                pass_copy((z + d) % zs).start()

            twin_copy(z * 2 + 1 - xl).start()

    busy = r < 3

    def hand_ring():
        @pl.loop(1, zs)
        def _(d):
            v = (z + d) % zs
            ring_arrival(v).wait_recv()
            twin_copy(v * 2 + xl).start()

    def hand_pass():
        @pl.loop(1, zs)
        def _(d):
            v = (z + d) % zs
            pass_arrival(v).wait_recv()
            twin_copy(v * 2 + 1 - xl).start()

    @pl.when(busy)
    def _():
        hand_ring()

    lists_copy.wait()
    marks_copy.wait()

    @pl.loop(r + 1, n_row)
    def _(g):
        up_arrival(g).wait_recv()

    @pl.loop(0, n_row)
    def _(g):
        for b in range(BP):
            put_operand(col_x, g * BP + b, col_raw[g, b])

    def products(which, operand, tiles, between):
        order_at, other_at = 2 * which, 2 * which + 1

        def body(s, total):
            between(s)
            for u in range(unroll):
                k = s * unroll + u
                t = lists_s[order_at, k]
                o = lists_s[other_at, k]
                term = jnp.dot(operand[o], tiles[t], preferred_element_type=F32)
                term = term[:width] + term[width:]
                total = total * marks_s[2 * which, k] + term * marks_s[2 * which + 1, k]
                running[k] = total
            return total

        lax.fori_loop(0, steps, body, jnp.zeros((width, TILE), F32))

    def hand_over(s):
        @pl.when(busy & (s == steps // 2))
        def _():
            hand_pass()

    products(0, col_x, turned, hand_over)

    @pl.loop(0, n_col)
    def _(p):
        for b in range(BP):
            k = lists_s[4, p * BP + b]
            row_part[p % 2, p // 2, b] = running[k] * marks_s[4, p * BP + b]

    def fold_copy(q):
        return remote(
            row_part.at[1 - core, q], from_twin.at[q], fold_send.at[q], fold_recv.at[q], r, twin
        )

    for d in range(1, chips + 1):
        fold_copy((chip + d) % chips).start()

    def back_copy(q):
        return remote(
            row_part.at[core, q],
            from_row.at[chip],
            back_send.at[q],
            back_recv.at[chip],
            r,
            q * 2 + core,
        )

    def back_arrival(q):
        return remote(
            from_row.at[q], from_row.at[q], back_send.at[0], back_recv.at[q], r, twin
        )

    def add_twin():
        @pl.loop(1, chips)
        def _(d):
            q = (chip + d) % chips
            fold_copy(q).wait_recv()
            row_part[core, q] = row_part[core, q] + from_twin[q]
            back_copy(q).start()

        fold_copy(chip).wait_recv()
        row_part[core, chip] = row_part[core, chip] + from_twin[chip]

    @pl.when(jnp.logical_not(busy))
    def _():
        add_twin()
        hand_ring()
        hand_pass()


    for q in range(chips):
        twin_arrival(q).wait_recv()

    @pl.loop(0, n_col)
    def _(p):
        for b in range(BP):
            put_operand(row_x, p * BP + b, row_raw[p, b])

    def fold_in(s):
        @pl.when(busy & (s == jnp.minimum(steps - 1, 1)))
        def _():
            add_twin()

    products(1, row_x, halves, fold_in)

    @pl.loop(0, n_row)
    def _(g):
        for b in range(BP):
            k = lists_s[5, g * BP + b]
            col_part[g, b] = running[k] * marks_s[5, g * BP + b]

    def down_copy(g):
        return remote(
            col_part.at[g], from_col.at[r], down_send.at[g], down_recv.at[r], g, c
        )

    def down_arrival(g):
        return remote(
            from_col.at[g], from_col.at[g], down_send.at[0], down_recv.at[g], r, twin
        )

    @pl.loop(0, n_row - 1 - r)
    def _(d):
        down_copy(n_row - 1 - d).start()

    row_part[core, chip] = row_part[core, chip] + col_part[r]
    for d in range(1, chips):
        q = (chip + d) % chips
        back_arrival(q).wait_recv()
        row_part[core, chip] = row_part[core, chip] + from_row[q]

    @pl.loop(0, r)
    def _(d):
        g = r - 1 - d
        down_arrival(g).wait_recv()
        row_part[core, chip] = row_part[core, chip] + from_col[g]

    for b in range(BP):
        out[:, b * TILE : (b + 1) * TILE] = row_part[core, chip, b]

    @pl.loop(0, r)
    def _(g):
        up_copy(g).wait_send()

    @pl.loop(r + 1, n_row)
    def _(g):
        down_copy(g).wait_send()

    @pl.loop(1, chips)
    def _(d):
        q = (chip + d) % chips
        back_copy(q).wait_send()

    side_copy().wait_send()

    @pl.loop(1, zs)
    def _(d):
        ring_copy((z + d) % zs).wait_send()
        pass_copy((z + d) % zs).wait_send()

    for q in range(chips):
        twin_copy(q).wait_send()
        fold_copy(q).wait_send()


def part_kernel(both, basis, residual):
    half = basis.shape[0]
    basis[...] = both[:half]
    residual[...] = both[half:]


def solution(mesh):
    n_row, n_col = mesh.shape["row"], mesh.shape["col"]
    chips = n_col // 2

    def local(ham_tiles, tile_list, tile_count, basis_block, residual_block):
        slots = ham_tiles.shape[2]
        width = 2 * basis_block.shape[0]
        padded = -(-slots // TILE) * TILE
        unroll = 80 if slots % 80 == 0 else 16
        chunks = 16
        ring = 4
        vmem = pl.BlockSpec(memory_space=pltpu.VMEM)
        dma = pltpu.SemaphoreType.DMA
        piece = (BP, width, TILE)
        whole = pl.BlockSpec(memory_space=pltpu.HBM)
        shape = jax.ShapeDtypeStruct(basis_block.shape, F32)
        both = pl.pallas_call(
            functools.partial(kernel, n_row, n_col, unroll, chunks),
            out_shape=jax.ShapeDtypeStruct((width, basis_block.shape[1]), F32),
            in_specs=[
                whole,
                pl.BlockSpec(memory_space=pltpu.SMEM),
                whole,
                whole,
                whole,
            ],
            out_specs=vmem,
            scratch_shapes=[
                pltpu.VMEM((ring, slots // chunks, TILE, TILE), F32),
                pltpu.VMEM((slots, 2 * TILE, TILE), BF),
                pltpu.VMEM((slots, 2 * TILE, TILE), BF),
                pltpu.VMEM((slots, width, TILE), F32),
                pltpu.VMEM((n_col,) + piece, F32),
                pltpu.VMEM((n_row,) + piece, F32),
                pltpu.VMEM((n_col * BP, 2 * width, 2 * TILE), BF),
                pltpu.VMEM((n_row * BP, 2 * width, 2 * TILE), BF),
                pltpu.VMEM((2, chips) + piece, F32),
                pltpu.VMEM((chips,) + piece, F32),
                pltpu.VMEM((chips,) + piece, F32),
                pltpu.VMEM((n_row,) + piece, F32),
                pltpu.VMEM((n_row,) + piece, F32),
                pltpu.VMEM((8, padded), I32),
                pltpu.SMEM((8, padded), I32),
                pltpu.VMEM((8, padded), F32),
                pltpu.SMEM((8, padded), F32),
                pltpu.VMEM((1, 1, 2, slots), I32),
                dma((2 * BP + 1,)),
                dma((ring,)),
                dma((2,)),
                pltpu.SemaphoreType.REGULAR,
                pltpu.SemaphoreType.REGULAR,
                dma((1,)),
                dma((1,)),
                dma((chips // 2,)),
                dma((chips // 2,)),
                dma((chips // 2,)),
                dma((chips // 2,)),
                dma((chips,)),
                dma((chips,)),
                dma((n_row,)),
                dma((n_row,)),
                dma((chips,)),
                dma((chips,)),
                dma((chips,)),
                dma((chips,)),
                dma((n_row,)),
                dma((n_row,)),
            ],
            compiler_params=pltpu.CompilerParams(
                collective_id=0,
                has_side_effects=True,
                vmem_limit_bytes=60 * 2**20,
            ),
        )(
            jnp.swapaxes(tile_list, 2, 3),
            tile_count,
            basis_block,
            residual_block,
            ham_tiles,
        )
        return pl.pallas_call(
            part_kernel,
            out_shape=(shape, shape),
            in_specs=[vmem],
            out_specs=(vmem, vmem),
        )(both)

    return jax.shard_map(
        local,
        mesh=mesh,
        in_specs=(
            P("row", "col", None, None, None),
            P("row", "col", None, None),
            P("row", "col"),
            P(None, ("row", "col")),
            P(None, ("row", "col")),
        ),
        out_specs=(P(None, ("row", "col")), P(None, ("row", "col"))),
        check_vma=False,
    )
```

```python
import functools

import jax
import jax.numpy as jnp
from jax import lax
from jax.experimental import pallas as pl
from jax.experimental.pallas import tpu as pltpu
from jax.sharding import PartitionSpec as P

MESH = pl.DeviceIdType.MESH
TILE = 128
BP = 4
BF = jnp.bfloat16
F32 = jnp.float32
I32 = jnp.int32


def split2(value):
    hi = value.astype(BF)
    lo = (value - hi.astype(F32)).astype(BF)
    return hi, lo


def put_operand(dst, index, block):
    rows = block.shape[0]
    hi, lo = split2(block)
    dst[index, :rows, :TILE] = hi
    dst[index, :rows, TILE:] = hi
    dst[index, rows:, :TILE] = lo
    dst[index, rows:, TILE:] = jnp.zeros_like(lo)


def row_of(column, spot):
    return jnp.sum(jnp.where(spot, column, 0), axis=0, keepdims=True)


def column_of(row, spot):
    return jnp.sum(jnp.where(spot, row, 0), axis=1, keepdims=True)


def sorted_lists(key, other, weight2, iota0, iota1, slots):
    tagged = key * 512 + iota0[:, :1]
    tagged_row = row_of(tagged, iota0 == iota1)
    before = (tagged_row < tagged) & (iota1 < slots)
    rank = jnp.sum(jnp.where(before, 1, 0), axis=1, keepdims=True)
    earlier = before & (tagged_row >= key * 512)
    repeats = jnp.minimum(
        jnp.sum(jnp.where(earlier, 1, 0), axis=1, keepdims=True), 1
    )
    place = rank == iota1
    return (
        row_of(iota0[:, :1], place),
        row_of(other, place),
        row_of(repeats, place),
        row_of(weight2, place),
    )


def segment_ends(key, lanes):
    last = jnp.sum(jnp.where(key <= lanes, 1, 0), axis=0, keepdims=True) - 1
    some = jnp.minimum(jnp.sum(jnp.where(key == lanes, 1, 0), axis=0, keepdims=True), 1)
    return jnp.maximum(last, 0), some


def kernel(
    n_row,
    n_col,
    unroll,
    chunks,
    list_ref,
    count_ref,
    basis_ref,
    residual_ref,
    tiles_ref,
    out,
    raw,
    halves,
    turned,
    running,
    row_raw,
    col_raw,
    row_x,
    col_x,
    row_part,
    from_twin,
    from_row,
    col_part,
    from_col,
    lists_v,
    lists_s,
    marks_v,
    marks_s,
    list_v,
    out_v,
    out_sem,
    own_sem,
    tile_sem,
    list_sem,
    near_sem,
    in_sem,
    side_send,
    side_recv,
    ring_send,
    ring_recv,
    pass_send,
    pass_recv,
    twin_send,
    twin_recv,
    up_send,
    up_recv,
    fold_send,
    fold_recv,
    back_send,
    back_recv,
    down_send,
    down_recv,
):
    slots = halves.shape[0]
    width = row_raw.shape[2]
    half = width // 2
    chips = n_col // 2
    per = slots // chunks
    ring = raw.shape[0]
    blocks = n_col * BP
    r = lax.axis_index("row")
    c = lax.axis_index("col")
    core = c % 2
    chip = c // 2
    twin = chip * 2 + 1 - core
    zs, z, xl = chips // 2, chip // 2, chip % 2
    side = (z * 2 + 1 - xl) * 2 + core

    upper = (n_row - 1 - r) * (BP * blocks) + BP * BP * c + BP * (BP + 1) // 2
    most = (n_row - 1) * (BP * blocks) + BP * BP * (n_col - 1) + BP * (BP + 1) // 2
    bound = jnp.minimum(slots * upper // most + 1, slots)
    steps = (bound + unroll - 1) // unroll
    parts = (steps * unroll + per - 1) // per

    def tile_copy(k):
        return pltpu.make_async_copy(
            tiles_ref.at[0, 0, pl.ds(k * per, per)], raw.at[k % ring], tile_sem.at[k % ring]
        )

    def remote(src, dst, send, recv, row, col):
        return pltpu.make_async_remote_copy(
            src_ref=src,
            dst_ref=dst,
            send_sem=send,
            recv_sem=recv,
            device_id=(row, col),
            device_id_type=MESH,
        )

    own = []
    for b in range(BP):
        columns = pl.ds(b * TILE, TILE)
        for k, ref in enumerate((basis_ref, residual_ref)):
            own.append(
                pltpu.make_async_copy(
                    ref.at[:, columns],
                    row_raw.at[c, b, pl.ds(k * half, half)],
                    own_sem.at[2 * b + k],
                )
            )
    own.append(pltpu.make_async_copy(list_ref, list_v, own_sem.at[2 * BP]))
    for copy in own:
        copy.start()

    @pl.loop(0, jnp.minimum(parts, ring))
    def _(k):
        tile_copy(k).start()

    for g in range(n_row):

        @pl.when(g < r)
        def _():
            col_raw[g] = jnp.zeros(col_raw.shape[1:], F32)

    barrier = pltpu.get_barrier_semaphore()

    @pl.loop(r + 1, n_row)
    def _(g):
        pl.semaphore_signal(barrier, inc=1, device_id=(g, c), device_id_type=MESH)

    @pl.loop(chip + 1, chips)
    def _(q):
        pl.semaphore_signal(
            barrier, inc=1, device_id=(r, q * 2 + core), device_id_type=MESH
        )

    @pl.when(core == 0)
    def _():
        pl.semaphore_signal(barrier, inc=1, device_id=(r, twin), device_id_type=MESH)

    @pl.when(r + chip + core > 0)
    def _():
        pl.semaphore_wait(barrier, r + chip + core)

    for copy in own[:-1]:
        copy.wait()

    @pl.loop(0, z * 2)
    def _(q):
        pl.semaphore_signal(
            in_sem, inc=1, device_id=(r, q * 2 + core), device_id_type=MESH
        )

    @pl.when(xl == 1)
    def _():
        pl.semaphore_signal(near_sem, inc=1, device_id=(r, side), device_id_type=MESH)

    @pl.when(core == 1)
    def _():
        pl.semaphore_signal(near_sem, inc=1, device_id=(r, twin), device_id_type=MESH)

    def up_copy(g):
        return remote(row_raw.at[c], col_raw.at[r], up_send.at[g], up_recv.at[r], g, c)

    def up_arrival(g):
        return remote(col_raw.at[g], col_raw.at[g], up_send.at[0], up_recv.at[g], r, twin)

    def side_copy():
        return remote(row_raw.at[c], row_raw.at[c], side_send.at[0], side_recv.at[0], r, side)

    def side_arrival():
        return remote(
            row_raw.at[side], row_raw.at[side], side_send.at[0], side_recv.at[0], r, side
        )

    def ring_copy(v):
        to = (v * 2 + xl) * 2 + core
        return remote(row_raw.at[c], row_raw.at[c], ring_send.at[v], ring_recv.at[z], r, to)

    def ring_arrival(v):
        piece = row_raw.at[(v * 2 + xl) * 2 + core]
        return remote(piece, piece, ring_send.at[0], ring_recv.at[v], r, side)

    def pass_copy(v):
        to = (v * 2 + xl) * 2 + core
        return remote(
            row_raw.at[side], row_raw.at[side], pass_send.at[v], pass_recv.at[z], r, to
        )

    def pass_arrival(v):
        piece = row_raw.at[(v * 2 + 1 - xl) * 2 + core]
        return remote(piece, piece, pass_send.at[0], pass_recv.at[v], r, side)

    def twin_copy(q):
        piece = row_raw.at[q * 2 + core]
        return remote(piece, piece, twin_send.at[q], twin_recv.at[q], r, twin)

    def twin_arrival(q):
        piece = row_raw.at[q * 2 + 1 - core]
        return remote(piece, piece, twin_send.at[0], twin_recv.at[q], r, twin)

    @pl.loop(0, r)
    def _(g):
        up_copy(g).start()

    @pl.when(core == 1)
    def _():
        twin_copy(chip).start()

    @pl.when(xl == 1)
    def _():
        side_copy().start()

    @pl.loop(0, z)
    def _(v):
        ring_copy(v).start()

    col_raw[r] = row_raw[c]
    own[-1].wait()

    padded = lists_v.shape[1]
    iota0 = lax.broadcasted_iota(I32, (slots, padded), 0)
    iota1 = lax.broadcasted_iota(I32, (slots, padded), 1)
    listing = jnp.concatenate(
        [list_v[0, 0], jnp.zeros((2, padded - slots), I32)], axis=1
    )
    local_row = column_of(listing[0:1], iota0 == iota1)
    local_col = column_of(listing[1:2], iota0 == iota1)
    live = iota0[:, :1] < count_ref[0, 0]
    diagonal = (r * (n_col * BP) + local_row) == (
        (local_col // BP) * (n_col * BP) + c * BP + local_col % BP
    )
    weight2 = jnp.where(live, jnp.where(diagonal, 1, 2), 0)
    row_key = jnp.where(live, local_row, blocks)
    col_key = jnp.where(live, local_col, blocks)
    by_row = sorted_lists(row_key, local_col, weight2, iota0, iota1, slots)
    by_col = sorted_lists(col_key, local_row, weight2, iota0, iota1, slots)
    lanes = lax.broadcasted_iota(I32, (slots, TILE), 1)
    row_end, row_some = segment_ends(row_key, lanes)
    col_end, col_some = segment_ends(col_key, lanes)
    for k, (order, other, again, weight) in enumerate((by_row, by_col)):
        lists_v[2 * k : 2 * k + 1] = order
        lists_v[2 * k + 1 : 2 * k + 2] = other
        marks_v[2 * k : 2 * k + 1] = again.astype(F32)
        marks_v[2 * k + 1 : 2 * k + 2] = weight.astype(F32) * 0.5
    lists_v[4:5, :TILE] = row_end
    lists_v[5:6, :TILE] = col_end
    marks_v[4:5, :TILE] = row_some.astype(F32)
    marks_v[5:6, :TILE] = col_some.astype(F32)
    lists_copy = pltpu.make_async_copy(lists_v, lists_s, list_sem.at[0])
    marks_copy = pltpu.make_async_copy(marks_v, marks_s, list_sem.at[1])
    lists_copy.start()
    marks_copy.start()

    group = min(per, 20)

    @pl.loop(0, parts)
    def _(k):
        tile_copy(k).wait()

        @pl.loop(0, per // group)
        def _(s):
            for u in range(group):
                at = s * group + u
                hi, lo = split2(raw[k % ring, at])
                t = k * per + at
                halves[t, :TILE] = hi
                halves[t, TILE:] = lo
                turned[t, :TILE] = hi.T
                turned[t, TILE:] = lo.T

        @pl.when(k + ring < parts)
        def _():
            tile_copy(k + ring).start()

        @pl.when(k == jnp.minimum(parts, 2) - 1)
        def _():
            @pl.when(1 - xl + 1 - core > 0)
            def _():
                pl.semaphore_wait(near_sem, 1 - xl + 1 - core)

            @pl.when(xl == 0)
            def _():
                side_copy().start()

            @pl.when(core == 0)
            def _():
                twin_copy(chip).start()

        @pl.when(k == jnp.minimum(parts, 6) - 1)
        def _():
            @pl.when(zs - 1 - z > 0)
            def _():
                pl.semaphore_wait(in_sem, 2 * (zs - 1 - z))

            @pl.loop(z + 1, zs)
            def _(v):
                ring_copy(v).start()

            side_arrival().wait_recv()

            @pl.loop(1, zs)
            def _(d):
                pass_copy((z + d) % zs).start()

            twin_copy(z * 2 + 1 - xl).start()

    busy = r < 3

    def hand_ring():
        @pl.loop(1, zs)
        def _(d):
            v = (z + d) % zs
            ring_arrival(v).wait_recv()
            twin_copy(v * 2 + xl).start()

    def hand_pass():
        @pl.loop(1, zs)
        def _(d):
            v = (z + d) % zs
            pass_arrival(v).wait_recv()
            twin_copy(v * 2 + 1 - xl).start()

    @pl.when(busy)
    def _():
        hand_ring()

    lists_copy.wait()
    marks_copy.wait()

    @pl.loop(r + 1, n_row)
    def _(g):
        up_arrival(g).wait_recv()

    @pl.loop(0, n_row)
    def _(g):
        for b in range(BP):
            put_operand(col_x, g * BP + b, col_raw[g, b])

    def products(which, operand, tiles, between):
        order_at, other_at = 2 * which, 2 * which + 1

        def body(s, total):
            between(s)
            for u in range(unroll):
                k = s * unroll + u
                t = lists_s[order_at, k]
                o = lists_s[other_at, k]
                term = jnp.dot(operand[o], tiles[t], preferred_element_type=F32)
                term = term[:width] + term[width:]
                total = total * marks_s[2 * which, k] + term * marks_s[2 * which + 1, k]
                running[k] = total
            return total

        lax.fori_loop(0, steps, body, jnp.zeros((width, TILE), F32))

    def hand_over(s):
        @pl.when(busy & (s == steps // 2))
        def _():
            hand_pass()

    products(0, col_x, turned, hand_over)

    @pl.loop(0, n_col)
    def _(p):
        for b in range(BP):
            k = lists_s[4, p * BP + b]
            row_part[p % 2, p // 2, b] = running[k] * marks_s[4, p * BP + b]

    def fold_copy(q):
        return remote(
            row_part.at[1 - core, q], from_twin.at[q], fold_send.at[q], fold_recv.at[q], r, twin
        )

    for d in range(1, chips + 1):
        fold_copy((chip + d) % chips).start()

    def back_copy(q):
        return remote(
            row_part.at[core, q],
            from_row.at[chip],
            back_send.at[q],
            back_recv.at[chip],
            r,
            q * 2 + core,
        )

    def back_arrival(q):
        return remote(
            from_row.at[q], from_row.at[q], back_send.at[0], back_recv.at[q], r, twin
        )

    def add_twin():
        @pl.loop(1, chips)
        def _(d):
            q = (chip + d) % chips
            fold_copy(q).wait_recv()
            row_part[core, q] = row_part[core, q] + from_twin[q]
            back_copy(q).start()

        fold_copy(chip).wait_recv()
        row_part[core, chip] = row_part[core, chip] + from_twin[chip]

    @pl.when(jnp.logical_not(busy))
    def _():
        add_twin()
        hand_ring()
        hand_pass()


    for q in range(chips):
        twin_arrival(q).wait_recv()

    @pl.loop(0, n_col)
    def _(p):
        for b in range(BP):
            put_operand(row_x, p * BP + b, row_raw[p, b])

    def fold_in(s):
        @pl.when(busy & (s == jnp.minimum(steps - 1, 1)))
        def _():
            add_twin()

    products(1, row_x, halves, fold_in)

    @pl.loop(0, n_row)
    def _(g):
        for b in range(BP):
            k = lists_s[5, g * BP + b]
            col_part[g, b] = running[k] * marks_s[5, g * BP + b]

    def down_copy(g):
        return remote(
            col_part.at[g], from_col.at[r], down_send.at[g], down_recv.at[r], g, c
        )

    def down_arrival(g):
        return remote(
            from_col.at[g], from_col.at[g], down_send.at[0], down_recv.at[g], r, twin
        )

    @pl.loop(0, n_row - 1 - r)
    def _(d):
        down_copy(n_row - 1 - d).start()

    row_part[core, chip] = row_part[core, chip] + col_part[r]
    for d in range(1, chips):
        q = (chip + d) % chips
        back_arrival(q).wait_recv()
        row_part[core, chip] = row_part[core, chip] + from_row[q]

    @pl.loop(0, r)
    def _(d):
        g = r - 1 - d
        down_arrival(g).wait_recv()
        row_part[core, chip] = row_part[core, chip] + from_col[g]

    for b in range(BP):
        out_v[:, b * TILE : (b + 1) * TILE] = row_part[core, chip, b]
    result = pltpu.make_async_copy(out_v, out, out_sem.at[0])
    result.start()

    @pl.loop(0, r)
    def _(g):
        up_copy(g).wait_send()

    @pl.loop(r + 1, n_row)
    def _(g):
        down_copy(g).wait_send()

    @pl.loop(1, chips)
    def _(d):
        q = (chip + d) % chips
        back_copy(q).wait_send()

    side_copy().wait_send()

    @pl.loop(1, zs)
    def _(d):
        ring_copy((z + d) % zs).wait_send()
        pass_copy((z + d) % zs).wait_send()

    for q in range(chips):
        twin_copy(q).wait_send()
        fold_copy(q).wait_send()
    result.wait()


def part_kernel(both, basis, residual):
    half = basis.shape[0]
    basis[...] = both[:half]
    residual[...] = both[half:]


def solution(mesh):
    n_row, n_col = mesh.shape["row"], mesh.shape["col"]
    chips = n_col // 2

    def local(ham_tiles, tile_list, tile_count, basis_block, residual_block):
        slots = ham_tiles.shape[2]
        width = 2 * basis_block.shape[0]
        padded = -(-slots // TILE) * TILE
        unroll = 80 if slots % 80 == 0 else 16
        chunks = 16
        ring = 4
        vmem = pl.BlockSpec(memory_space=pltpu.VMEM)
        dma = pltpu.SemaphoreType.DMA
        piece = (BP, width, TILE)
        whole = pl.BlockSpec(memory_space=pltpu.HBM)
        shape = jax.ShapeDtypeStruct(basis_block.shape, F32)
        both = pl.pallas_call(
            functools.partial(kernel, n_row, n_col, unroll, chunks),
            out_shape=jax.ShapeDtypeStruct((width, basis_block.shape[1]), F32),
            in_specs=[
                whole,
                pl.BlockSpec(memory_space=pltpu.SMEM),
                whole,
                whole,
                whole,
            ],
            out_specs=whole,
            scratch_shapes=[
                pltpu.VMEM((ring, slots // chunks, TILE, TILE), F32),
                pltpu.VMEM((slots, 2 * TILE, TILE), BF),
                pltpu.VMEM((slots, 2 * TILE, TILE), BF),
                pltpu.VMEM((slots, width, TILE), F32),
                pltpu.VMEM((n_col,) + piece, F32),
                pltpu.VMEM((n_row,) + piece, F32),
                pltpu.VMEM((n_col * BP, 2 * width, 2 * TILE), BF),
                pltpu.VMEM((n_row * BP, 2 * width, 2 * TILE), BF),
                pltpu.VMEM((2, chips) + piece, F32),
                pltpu.VMEM((chips,) + piece, F32),
                pltpu.VMEM((chips,) + piece, F32),
                pltpu.VMEM((n_row,) + piece, F32),
                pltpu.VMEM((n_row,) + piece, F32),
                pltpu.VMEM((8, padded), I32),
                pltpu.SMEM((8, padded), I32),
                pltpu.VMEM((8, padded), F32),
                pltpu.SMEM((8, padded), F32),
                pltpu.VMEM((1, 1, 2, slots), I32),
                pltpu.VMEM((width, basis_block.shape[1]), F32),
                dma((1,)),
                dma((2 * BP + 1,)),
                dma((ring,)),
                dma((2,)),
                pltpu.SemaphoreType.REGULAR,
                pltpu.SemaphoreType.REGULAR,
                dma((1,)),
                dma((1,)),
                dma((chips // 2,)),
                dma((chips // 2,)),
                dma((chips // 2,)),
                dma((chips // 2,)),
                dma((chips,)),
                dma((chips,)),
                dma((n_row,)),
                dma((n_row,)),
                dma((chips,)),
                dma((chips,)),
                dma((chips,)),
                dma((chips,)),
                dma((n_row,)),
                dma((n_row,)),
            ],
            compiler_params=pltpu.CompilerParams(
                collective_id=0,
                has_side_effects=True,
                vmem_limit_bytes=60 * 2**20,
            ),
        )(
            jnp.swapaxes(tile_list, 2, 3),
            tile_count,
            basis_block,
            residual_block,
            ham_tiles,
        )
        return pl.pallas_call(
            part_kernel,
            out_shape=(shape, shape),
            in_specs=[vmem],
            out_specs=(vmem, vmem),
        )(both)

    return jax.shard_map(
        local,
        mesh=mesh,
        in_specs=(
            P("row", "col", None, None, None),
            P("row", "col", None, None),
            P("row", "col"),
            P(None, ("row", "col")),
            P(None, ("row", "col")),
        ),
        out_specs=(P(None, ("row", "col")), P(None, ("row", "col"))),
        check_vma=False,
    )
```
